32 devices in a mesh: narrow: 8 (over z, y), wide: 4 (over x, core).
Axes of the slice: x: 2, y: 2, z: 4, core: 2. Of those that a mesh axis runs over, the one named last changes fastest.
Arguments:
- tokens: bfloat16 [2048, 2, 2048], P(('narrow', 'wide')), may hold values from -6 to 6
- lengths: int32 [2], replicated, may hold values from 64 to 2048, as said below
- attn_gain: float32 [2048], replicated, may hold values from 0.1 to 1.9
- w_query: bfloat16 [2048, 2048], P(None, 'wide'), may hold values from -0.125 to 0.125
- key_matrix: bfloat16 [2048, 512], P(None, 'wide'), may hold values from -0.125 to 0.125
- value_matrix: bfloat16 [2048, 512], P(None, 'wide'), may hold values from -0.125 to 0.125
- q_gain: float32 [64], replicated, may hold values from 0.1 to 1.9
- k_gain: float32 [64], replicated, may hold values from 0.1 to 1.9
- w_out: bfloat16 [2048, 2048], P('wide'), may hold values from -1 to 1
- ffn_gain: float32 [2048], replicated, may hold values from 0.1 to 1.9
- w_gate: bfloat16 [2048, 8192], P(None, 'wide'), may hold values from -0.125 to 0.125
- w_up: bfloat16 [2048, 8192], P(None, 'wide'), may hold values from -0.125 to 0.125
- w_down: bfloat16 [8192, 2048], P('wide'), may hold values from -0.0625 to 0.0625
- out_grad: bfloat16 [2048, 2, 2048], P(('narrow', 'wide')), may hold values from -6 to 6
Outputs:
- mixed: bfloat16 [2048, 2, 2048], P(('narrow', 'wide'))
- d_tokens: float32 [2048, 2, 2048], P(('narrow', 'wide'))
- d_attn_gain: float32 [2048], replicated
- d_w_query: float32 [2048, 2048], P('narrow', 'wide')
- d_w_key: float32 [2048, 512], P('narrow', 'wide')
- d_w_value: float32 [2048, 512], P('narrow', 'wide')
- d_q_gain: float32 [64], replicated
- d_k_gain: float32 [64], replicated
- d_w_out_t: float32 [2048, 2048], P('narrow', 'wide')
- d_ffn_gain: float32 [2048], replicated
- d_w_gate: float32 [2048, 8192], P('narrow', 'wide')
- d_w_up: float32 [2048, 8192], P('narrow', 'wide')
- d_w_down_t: float32 [2048, 8192], P('narrow', 'wide')
The draws below stay inside these ranges and needn't reach their ends.
Inputs may be any that keep to these rules, and one draw needn't show every extreme that they name: `lengths`: in every draw one row, drawn from the seed, uses all 2048 slots; the others are mostly short.
All inputs are finite; a program needn't handle non-finite values.
Results may differ from the reference program's by a relative error of at most 0.02.
Values may be sent and summed in bfloat16 or wider, within the bound.
No kernel may reach another device: no remote copies, remote signals or barrier semaphores. Data moves between devices by JAX's collectives and lax.ppermute only.
A program may use at most 256 MiB of HBM per device.

```python
import math
import jax
import jax.numpy as jnp
from jax import lax

MODEL_WIDTH = 2048
QUERY_HEADS = 32
KEY_VALUE_HEADS = 8
HEAD_WIDTH = 64
FF = 8192
ROW_SLOTS = 2048
ROW_COUNT = 2


def draw_lengths(key, part):
    key = jax.random.fold_in(key, 11)
    first_key, second_key, row_key = jax.random.split(key, 3)
    least = ROW_SLOTS // 32
    span = ROW_SLOTS - least
    first = jax.random.randint(first_key, (ROW_COUNT,), 0, 65)
    second = jax.random.randint(second_key, (ROW_COUNT,), 0, 65)
    drawn = least + span * first * second // 4096
    full_row = jax.random.randint(row_key, (), 0, ROW_COUNT)
    return jnp.where(jnp.arange(ROW_COUNT) == full_row, ROW_SLOTS, drawn).astype(jnp.int32)


def steps_of(own_key, extent, shards, smallest, largest):
    level, own = 1.0, jax.random.fold_in(own_key, 6)
    for axis_at, parts in shards:
        draws = jnp.exp(jax.random.uniform(jax.random.fold_in(own, axis_at), (parts,), jnp.float32, smallest / len(shards), largest / len(shards)))
        level = level * jnp.repeat(draws, extent[axis_at] // parts).reshape([-1 if axis == axis_at else 1 for axis in range(len(extent))])
    return level


def noise(key, dims, width, bound, cuts=(), kind=jnp.bfloat16):
    level = steps_of(key, dims, cuts, -0.22, 0.18) if cuts else 1.0
    entries = jax.random.normal(key, dims, jnp.float32) * width * level
    return jnp.minimum(jnp.maximum(entries, -bound), bound).astype(kind)


def setup_inputs(seed: int = 0) -> dict:
    key_of = jax.random.split(jax.random.key(seed), 15)
    return {
        "tokens": noise(key_of[0], (ROW_SLOTS, ROW_COUNT, MODEL_WIDTH), 1.0, 6.0, ((0, 32),)),
        "lengths": draw_lengths(jax.random.fold_in(key_of[14], 71), 0),
        "attn_gain": jnp.clip(1.0 + 0.18 * jax.random.normal(key_of[2], (MODEL_WIDTH,), jnp.float32), 0.1, 1.9),
        "w_query": noise(key_of[3], (MODEL_WIDTH, QUERY_HEADS * HEAD_WIDTH), MODEL_WIDTH ** -0.5, 0.125, ((1, 4),)),
        "key_matrix": noise(key_of[4], (MODEL_WIDTH, KEY_VALUE_HEADS * HEAD_WIDTH), MODEL_WIDTH ** -0.5, 0.125, ((1, 4),)),
        "value_matrix": noise(key_of[5], (MODEL_WIDTH, KEY_VALUE_HEADS * HEAD_WIDTH), MODEL_WIDTH ** -0.5, 0.125, ((1, 4),)),
        "q_gain": jnp.clip(1.0 + 0.18 * jax.random.normal(key_of[6], (HEAD_WIDTH,), jnp.float32), 0.1, 1.9),
        "k_gain": jnp.clip(1.0 + 0.18 * jax.random.normal(key_of[7], (HEAD_WIDTH,), jnp.float32), 0.1, 1.9),
        "w_out": noise(key_of[8], (QUERY_HEADS * HEAD_WIDTH, MODEL_WIDTH), (QUERY_HEADS * HEAD_WIDTH // 64) ** -0.5, 1.0, ((0, 4),)),
        "ffn_gain": jnp.clip(1.0 + 0.18 * jax.random.normal(key_of[9], (MODEL_WIDTH,), jnp.float32), 0.1, 1.9),
        "w_gate": noise(key_of[10], (MODEL_WIDTH, FF), MODEL_WIDTH ** -0.5, 0.125, ((1, 4),)),
        "w_up": noise(key_of[11], (MODEL_WIDTH, FF), MODEL_WIDTH ** -0.5, 0.125, ((1, 4),)),
        "w_down": noise(key_of[12], (FF, MODEL_WIDTH), FF ** -0.5, 0.0625, ((0, 4),)),
        "out_grad": noise(key_of[13], (ROW_SLOTS, ROW_COUNT, MODEL_WIDTH), 1.0, 6.0, ((0, 32),)),
    }


EPS = 1e-06
NEG = -1e+30
HIGH = lax.Precision.HIGHEST

@jax.custom_vjp
def reduced_precision(v):
    return lax.optimization_barrier(v.astype(jnp.bfloat16)).astype(jnp.float32)

@jax.custom_vjp
def low_back(v):
    return v

def low_keep(v):
    return (reduced_precision(v), None)

def low_pass(kept, grad):
    return (grad,)

def back_keep(v):
    return (v, None)

def back_low(kept, grad):
    return (reduced_precision(grad),)
reduced_precision.defvjp(low_keep, low_pass)
low_back.defvjp(back_keep, back_low)

def rows_normalize(value_rows, gain):
    return value_rows * lax.rsqrt(lax.optimization_barrier(jnp.mean(value_rows * value_rows, axis=-1, keepdims=True)) + EPS) * gain

def rotary_tables(positions, head_size):
    half = head_size // 2
    freqs = jnp.exp(-math.log(10000.0) * jnp.arange(half, dtype=jnp.float32) * 2.0 / head_size)
    angles = positions.astype(jnp.float32)[:, None] * freqs[None, :]
    return (jnp.cos(angles), jnp.sin(angles))

def rotary_apply(value_rows, cosine_table, sine_table):
    half = value_rows.shape[-1] // 2
    first = value_rows[..., :half]
    second = value_rows[..., half:]
    cos_b = cosine_table[:, None, None, :]
    sin_b = sine_table[:, None, None, :]
    return jnp.concatenate([first * cos_b - second * sin_b, second * cos_b + first * sin_b], axis=-1)

def attend(query, key_rows, value_rows, lengths):
    query_group = QUERY_HEADS // KEY_VALUE_HEADS
    block = min(512, ROW_SLOTS)
    starts = jnp.arange(ROW_SLOTS // block, dtype=jnp.int32) * block
    key_positions = jnp.arange(ROW_SLOTS, dtype=jnp.int32)
    scale = HEAD_WIDTH ** (-0.5)

    def one_sequence(item):
        query_s, key_s, value_s, length = item
        key_s = jnp.repeat(key_s, query_group, axis=1)
        value_s = jnp.repeat(value_s, query_group, axis=1)

        def one_block(start):
            query_b = lax.dynamic_slice_in_dim(query_s, start, block, 0)
            scores = jnp.einsum('qhd,khd->hqk', query_b, key_s, precision=HIGH) * scale
            scores = low_back(scores)
            query_positions = start + jnp.arange(block, dtype=jnp.int32)
            allowed = (key_positions[None, :] <= query_positions[:, None]) & (key_positions[None, :] < length)
            scores = jnp.where(allowed[None], scores, NEG)
            peak = lax.optimization_barrier(jnp.max(scores, axis=-1, keepdims=True))
            expo = jnp.exp(scores - peak)
            probs = expo / lax.optimization_barrier(jnp.sum(expo, axis=-1, keepdims=True))
            return jnp.einsum('hqk,khd->qhd', reduced_precision(probs), value_s, precision=HIGH)
        blocks = lax.map(jax.checkpoint(one_block), starts)
        return blocks.reshape(ROW_SLOTS, QUERY_HEADS, HEAD_WIDTH)
    mixed = lax.map(one_sequence, (jnp.moveaxis(query, 1, 0), jnp.moveaxis(key_rows, 1, 0), jnp.moveaxis(value_rows, 1, 0), lengths))
    return jnp.moveaxis(mixed, 0, 1)

def reference(tokens, lengths, attn_gain, w_query, key_matrix, value_matrix, q_gain, k_gain, w_out, ffn_gain, w_gate, w_up, w_down, out_grad):
    floats = [a.astype(jnp.float32) for a in (tokens, attn_gain, w_query, key_matrix, value_matrix, q_gain, k_gain, w_out, ffn_gain, w_gate, w_up, w_down)]

    def forward(inputs, attn_g, wq, wk, wv, q_g, key_gain_vector, wo, ffn_g, wg, wu, wd):
        rows = inputs.reshape(ROW_SLOTS * ROW_COUNT, MODEL_WIDTH)
        normed = reduced_precision(rows_normalize(rows, attn_g))
        query_raw = low_back(jnp.dot(normed, wq, precision=HIGH))
        key_unnormed = low_back(jnp.dot(normed, wk, precision=HIGH))
        value_unnormed = low_back(jnp.dot(normed, wv, precision=HIGH))
        cosine_table, sine_table = rotary_tables(jnp.arange(ROW_SLOTS, dtype=jnp.int32), HEAD_WIDTH)
        query = reduced_precision(rotary_apply(rows_normalize(query_raw.reshape(ROW_SLOTS, ROW_COUNT, QUERY_HEADS, HEAD_WIDTH), q_g), cosine_table, sine_table))
        key_rows = reduced_precision(rotary_apply(rows_normalize(key_unnormed.reshape(ROW_SLOTS, ROW_COUNT, KEY_VALUE_HEADS, HEAD_WIDTH), key_gain_vector), cosine_table, sine_table))
        value_rows = reduced_precision(value_unnormed.reshape(ROW_SLOTS, ROW_COUNT, KEY_VALUE_HEADS, HEAD_WIDTH))
        heads = attend(query, key_rows, value_rows, lengths)
        heads = reduced_precision(low_back(heads.reshape(ROW_SLOTS * ROW_COUNT, QUERY_HEADS * HEAD_WIDTH)))
        attn = low_back(jnp.dot(heads, wo, precision=HIGH))
        middle = rows + attn
        mid_normed = reduced_precision(rows_normalize(middle, ffn_g))
        gate = low_back(jnp.dot(mid_normed, wg, precision=HIGH))
        up = low_back(jnp.dot(mid_normed, wu, precision=HIGH))
        hidden = reduced_precision(jax.nn.silu(gate) * up)
        result = middle + jnp.dot(hidden, wd, precision=HIGH)
        return result.reshape(ROW_SLOTS, ROW_COUNT, MODEL_WIDTH)
    result, pull = jax.vjp(forward, *floats)
    valid = (jnp.arange(ROW_SLOTS, dtype=jnp.int32)[:, None] < lengths[None, :]).astype(jnp.float32)
    cotangent = out_grad.astype(jnp.float32) * valid[:, :, None]
    grads = pull(cotangent)
    return (result.astype(jnp.bfloat16), grads[0], grads[1], grads[2], grads[3], grads[4], grads[5], grads[6], grads[7].T, grads[8], grads[9], grads[10], grads[11].T)
```

```python
import functools
import math

import jax
import jax.numpy as jnp
from jax import lax
from jax.experimental import pallas as pl
from jax.experimental.pallas import tpu as pltpu
from jax.sharding import PartitionSpec as P

QUERY_HEADS = 32
KEY_VALUE_HEADS = 8
HEAD = 64
HALF = HEAD // 2
GROUP = QUERY_HEADS // KEY_VALUE_HEADS
EPS = 1e-06
SCALE = HEAD ** (-0.5)
AXES = ("narrow", "wide")
TP_BIT = 2
BF = jnp.bfloat16
F32 = jnp.float32
VMEM = 56 * 1024 * 1024

NN = (((1,), (0,)), ((), ()))
NT = (((1,), (1,)), ((), ()))
TN = (((0,), (0,)), ((), ()))


def mm(a, b, dims=NN):
    return lax.dot_general(a, b, dims, preferred_element_type=F32)


def cost(flops, nbytes, trans=0):
    return pl.CostEstimate(flops=int(flops), bytes_accessed=int(nbytes), transcendentals=int(trans))


class Line:
    def __init__(self, at):
        self.at = at
        self.last = []

    def call(self, kernel, *args, grid, in_specs, out_specs, out_shape, scratch=(), cost=None, name=None, deps=()):
        extra = [*self.last, *deps]

        def body(at_ref, *refs):
            kernel(at_ref, *refs[len(extra) :])

        outs = pl.pallas_call(
            body,
            grid_spec=pltpu.PrefetchScalarGridSpec(
                num_scalar_prefetch=1,
                grid=grid,
                in_specs=[pl.BlockSpec(memory_space=pl.ANY)] * len(extra) + list(in_specs),
                out_specs=out_specs,
                scratch_shapes=scratch,
            ),
            out_shape=out_shape,
            compiler_params=pltpu.CompilerParams(vmem_limit_bytes=VMEM),
            cost_estimate=cost,
            name=name,
        )(self.at, *extra, *args)
        self.last = [outs[0] if isinstance(outs, (list, tuple)) else outs]
        return outs


def key_block_mask(j):
    rows = j >> 1
    return (rows & 1) | ((j & 1) << 1) | ((rows >> 1) << 2)


def position_inside(t, share, w):
    u = t // share
    return ((((u & 1) << 1) | (u >> 1)) ^ w) * share + t % share


def positions_in_block(size, share, w, axis):
    shape = (size, 1) if axis == 0 else (1, size)
    return position_inside(lax.broadcasted_iota(jnp.int32, shape, axis), share, w)


def constant(shape):
    return pl.BlockSpec(shape, lambda *_: (0,) * len(shape))


def per_block(shape):
    return pl.BlockSpec(shape, lambda g, i, at: (g, i) + (0,) * (len(shape) - 2))


def per_sequence(shape):
    return pl.BlockSpec(shape, lambda g, *_: (g,) + (0,) * (len(shape) - 1))


def shape_of(shape, dtype=BF):
    return jax.ShapeDtypeStruct(shape, dtype)


def project_kernel(at_ref, a_ref, b_ref, wt_ref, cos_ref, sin_ref, qg_ref, kg_ref, kv_ref, q_ref, raw_ref):
    x = jnp.concatenate([a_ref[0], b_ref[0]], axis=0)
    y = mm(wt_ref[...], x, NT)
    heads = q_ref.shape[2]
    width = heads * HEAD
    raw_ref[0, 0] = y[: width + HEAD]
    c, s = cos_ref[0], sin_ref[0]

    def norm_rope(v, gain):
        r = lax.rsqrt(jnp.mean(v * v, axis=0, keepdims=True) + EPS)
        n = v * r * gain
        a, b = n[:HALF], n[HALF:]
        return a * c - b * s, b * c + a * s

    for h in range(heads):
        a, b = norm_rope(y[h * HEAD : (h + 1) * HEAD], qg_ref[...])
        q_ref[0, 0, h] = (jnp.concatenate([a, b], axis=0) * SCALE).astype(BF)
    a, b = norm_rope(y[width : width + HEAD], kg_ref[...])
    kv = jnp.concatenate([a, b, y[width + HEAD :]], axis=0)
    kv_ref[0] = kv.T.astype(BF)


def project(line, xn, wt, cos, sin, q_gain, k_gain):
    g, b, m = xn[0].shape
    c = wt.shape[0]
    heads = c // HEAD - 2
    table = pl.BlockSpec((1, HALF, b), lambda g, i, at: (i, 0, 0))
    return line.call(
        project_kernel, *xn, wt, cos, sin, q_gain, k_gain,
        grid=(g, 2),
        in_specs=[per_block((1, b // 2, m))] * 2
        + [constant((c, m)), table, table, constant((HEAD, 1)), constant((HEAD, 1))],
        out_specs=[
            per_block((1, b, 2 * HEAD)),
            per_block((1, 1, heads, HEAD, b)),
            per_block((1, 1, (heads + 1) * HEAD, b)),
        ],
        out_shape=[
            shape_of((g, 2 * b, 2 * HEAD)),
            shape_of((g, 2, heads, HEAD, b)),
            shape_of((g, 2, (heads + 1) * HEAD, b), F32),
        ],
        cost=cost(4 * g * b * m * c, 4 * g * b * m + 2 * c * m + 16 * g * b * c),
        name="project",
    )


def attend_kernel(count, share, at_ref, q_ref, *refs):
    kv_refs = refs[:count]
    wo_ref, pb_ref, pa_ref, oa_ref, ob_ref, log_ref, acc_ref, sum_ref = refs[count:]
    n, w = at_ref[0], at_ref[1]
    length = at_ref[3 + pl.program_id(0)]
    heads, _, b = q_ref.shape[2:]
    nq = n ^ (TP_BIT * pl.program_id(1))
    bound = jnp.minimum(nq * b + positions_in_block(b, share, w, 1), length - 1)
    acc_ref[...] = jnp.zeros_like(acc_ref)
    sum_ref[...] = jnp.zeros_like(sum_ref)
    inside = positions_in_block(b, share, w, 0)

    for k, kv_ref in enumerate(kv_refs):
        for tp in range(2):
            nk = n ^ key_block_mask(2 * k + tp)

            @pl.when((nk <= nq) & (nk * b < length))
            def _():
                kv = kv_ref[0, tp * b : (tp + 1) * b, :]
                allowed = nk * b + inside <= bound
                for h in range(heads):
                    scores = mm(kv[:, :HEAD], q_ref[0, 0, h])
                    p = jnp.where(allowed, jnp.exp(scores), 0.0)
                    sum_ref[h : h + 1] += jnp.sum(p, axis=0, keepdims=True)
                    acc_ref[h] += mm(kv, p.astype(BF), TN)

    outs = []
    for h in range(heads):
        total = sum_ref[h : h + 1]
        outs.append(acc_ref[h, HEAD:, :] / total)
    log_ref[0, 0] = jnp.log(sum_ref[...])
    o = jnp.concatenate(outs, axis=0).T.astype(BF)
    oa_ref[0] = o[: b // 2]
    ob_ref[0] = o[b // 2 :]
    part = mm(o, wo_ref[...]).astype(BF)
    pa_ref[0] = part[: b // 2]
    pb_ref[0] = part[b // 2 :]


def attend(line, q, kvs, w_out, share):
    g, _, heads, _, b = q.shape
    keys = 2 * b * len(kvs)
    m = w_out.shape[1]
    width = heads * HEAD
    return line.call(
        functools.partial(attend_kernel, len(kvs), share), q, *kvs, w_out,
        grid=(g, 2),
        in_specs=[per_block((1, 1, heads, HEAD, b))]
        + [per_sequence((1, 2 * b, 2 * HEAD))] * len(kvs)
        + [pl.BlockSpec((width, m), lambda g, i, at: (at[2], 0))],
        out_specs=[per_block((1, b // 2, m))] * 2
        + [per_block((1, b // 2, width))] * 2
        + [per_block((1, 1, heads, b))],
        out_shape=[shape_of((g, b, m))] * 2
        + [shape_of((g, b, width))] * 2
        + [shape_of((g, 2, heads, b), F32)],
        scratch=[pltpu.VMEM((heads, 2 * HEAD, b), F32), pltpu.VMEM((heads, b), F32)],
        cost=cost(
            2 * g * 2 * b * keys * heads * 192 + 4 * g * b * width * m,
            2 * g * (keys * 2 * HEAD + 2 * b * m) + 2 * width * m,
            g * b * keys * heads,
        ),
        name="attend",
    )


def attend_back_kernel(count, share, at_ref, dha_ref, dhb_ref, q_ref, *refs):
    kv_refs, refs = refs[:count], refs[count:]
    wo_ref, oa_ref, ob_ref, log_ref, raw_ref, cos_ref, sin_ref, qg_ref, dqa_ref, dqb_ref = refs[:10]
    dkv_refs, dqg_ref = refs[10 : 10 + count], refs[10 + count]
    q_ext, do_ext, delta, dq_acc, dkv_acc = refs[11 + count :]
    n, w = at_ref[0], at_ref[1]
    at_g, i = pl.program_id(0), pl.program_id(1)
    length = at_ref[3 + at_g]
    heads, _, b = q_ref.shape[2:]
    nq = n ^ (TP_BIT * i)
    bound = jnp.minimum(nq * b + positions_in_block(b, share, w, 1), length - 1)
    inside = positions_in_block(b, share, w, 0)

    @pl.when(i == 0)
    def _():
        dkv_acc[...] = jnp.zeros_like(dkv_acc)

    @pl.when((i == 0) & (at_g == 0))
    def _():
        dqg_ref[...] = jnp.zeros_like(dqg_ref)

    dh = jnp.concatenate([dha_ref[0], dhb_ref[0]], axis=0)
    do = mm(wo_ref[...], dh, NT).astype(BF)
    o = jnp.concatenate([oa_ref[0], ob_ref[0]], axis=0).astype(F32).T
    none = jnp.zeros((HEAD, b), BF)
    for h in range(heads):
        do_h = do[h * HEAD : (h + 1) * HEAD]
        o_h = o[h * HEAD : (h + 1) * HEAD]
        delta[h : h + 1] = jnp.sum(do_h.astype(F32) * o_h, axis=0, keepdims=True)
        do_ext[h] = jnp.concatenate([none, do_h], axis=0)
        q_ext[h] = jnp.concatenate([q_ref[0, 0, h], none], axis=0)
    dq_acc[...] = jnp.zeros_like(dq_acc)

    for k, kv_ref in enumerate(kv_refs):
        for tp in range(2):
            nk = n ^ key_block_mask(2 * k + tp)

            @pl.when((nk <= nq) & (nk * b < length) & (nq * b < length))
            def _():
                kv = kv_ref[0, tp * b : (tp + 1) * b, :]
                allowed = nk * b + inside <= bound
                total = jnp.zeros((b, 2 * HEAD), F32)
                for h in range(heads):
                    scores = mm(kv, q_ext[h])
                    p = jnp.where(allowed, jnp.exp(scores - log_ref[0, 0, h : h + 1]), 0.0)
                    dp = mm(kv, do_ext[h])
                    ds = (p * (dp - delta[h : h + 1])).astype(BF)
                    dq_acc[h] += mm(kv, ds, TN)
                    total += mm(ds, q_ext[h], NT) + mm(p.astype(BF), do_ext[h], NT)
                rows = (2 * k + tp) * b
                dkv_acc[rows : rows + b, :] += total

    c, s = cos_ref[0], sin_ref[0]
    parts = []
    gain_sum = jnp.zeros((HEAD, b), F32)
    for h in range(heads):
        dq = dq_acc[h, :HEAD, :] * SCALE
        e1, e2 = dq[:HALF], dq[HALF:]
        e = jnp.concatenate([e1 * c + e2 * s, e2 * c - e1 * s], axis=0)
        v = raw_ref[0, 0, h * HEAD : (h + 1) * HEAD, :]
        r = lax.rsqrt(jnp.mean(v * v, axis=0, keepdims=True) + EPS)
        unit = v * r
        ge = qg_ref[...] * e
        parts.append(r * (ge - unit * jnp.mean(ge * unit, axis=0, keepdims=True)))
        gain_sum += e * unit
    dq = jnp.concatenate(parts, axis=0).T.astype(BF)
    dqa_ref[0] = dq[: b // 2]
    dqb_ref[0] = dq[b // 2 :]
    dqg_ref[...] += gain_sum

    @pl.when(i == 1)
    def _():
        for k, ref in enumerate(dkv_refs):
            ref[0] = dkv_acc[2 * k * b : 2 * (k + 1) * b, :].astype(BF)


def attend_back(line, dh, q, kvs, w_out, o, log, raw, cos, sin, q_gain, share):
    g, _, heads, _, b = q.shape
    keys = 2 * b * len(kvs)
    m = w_out.shape[1]
    width = heads * HEAD
    half_rows = per_block((1, b // 2, width))
    table = pl.BlockSpec((1, HALF, b), lambda g, i, at: (i, 0, 0))
    return line.call(
        functools.partial(attend_back_kernel, len(kvs), share),
        *dh, q, *kvs, w_out, *o, log, raw, cos, sin, q_gain,
        grid=(g, 2),
        in_specs=[per_block((1, b // 2, m))] * 2
        + [per_block((1, 1, heads, HEAD, b))]
        + [per_sequence((1, 2 * b, 2 * HEAD))] * len(kvs)
        + [
            pl.BlockSpec((width, m), lambda g, i, at: (at[2], 0)),
            half_rows,
            half_rows,
            per_block((1, 1, heads, b)),
            per_block((1, 1, width, b)),
            table,
            table,
            constant((HEAD, 1)),
        ],
        out_specs=[half_rows, half_rows]
        + [per_sequence((1, 2 * b, 2 * HEAD))] * len(kvs)
        + [constant((HEAD, b))],
        scratch=[
            pltpu.VMEM((heads, 2 * HEAD, b), BF),
            pltpu.VMEM((heads, 2 * HEAD, b), BF),
            pltpu.VMEM((heads, b), F32),
            pltpu.VMEM((heads, 2 * HEAD, b), F32),
            pltpu.VMEM((keys, 2 * HEAD), F32),
        ],
        out_shape=[shape_of((g, b, width))] * 2
        + [shape_of((g, 2 * b, 2 * HEAD))] * len(kvs)
        + [shape_of((HEAD, b), F32)],
        cost=cost(
            2 * g * 2 * b * keys * heads * 640 + 4 * g * b * width * m,
            2 * g * (keys * 4 * HEAD + 2 * b * m) + 2 * width * m,
            g * b * keys * heads,
        ),
        name="attend_back",
    )


def project_back_kernel(count, at_ref, *refs):
    dkv_refs = refs[:count]
    (
        dqa_ref, dqb_ref, raw_ref, xa_ref, xb_ref, wt_ref, cos_ref, sin_ref, kg_ref,
        dxb_ref, dxa_ref, dkva_ref, dkvb_ref, dkg_ref, dag_ref,
    ) = refs[count:]

    @pl.when((pl.program_id(0) == 0) & (pl.program_id(1) == 0))
    def _():
        dkg_ref[...] = jnp.zeros_like(dkg_ref)
        dag_ref[...] = jnp.zeros_like(dag_ref)

    total = dkv_refs[0][0].astype(F32)
    for ref in dkv_refs[1:]:
        total += ref[0].astype(F32)
    t = total.T
    half = total.shape[0] // 2
    c, s = cos_ref[0], sin_ref[0]
    e1, e2 = t[:HALF], t[HALF:HEAD]
    e = jnp.concatenate([e1 * c + e2 * s, e2 * c - e1 * s], axis=0)
    v = raw_ref[0, 0]
    r = lax.rsqrt(jnp.mean(v * v, axis=0, keepdims=True) + EPS)
    unit = v * r
    ge = kg_ref[...] * e
    dk = r * (ge - unit * jnp.mean(ge * unit, axis=0, keepdims=True))
    dkg_ref[...] += e * unit
    dkv = jnp.concatenate([dk, t[HEAD:]], axis=0).T.astype(BF)
    dkva_ref[0] = dkv[:half]
    dkvb_ref[0] = dkv[half:]
    width = dqa_ref.shape[2]
    gain_sum = jnp.zeros(dag_ref.shape, F32)
    for rows, dq_ref, x_ref, dx_ref in (
        (slice(0, half), dqa_ref, xa_ref, dxa_ref),
        (slice(half, 2 * half), dqb_ref, xb_ref, dxb_ref),
    ):
        dx = mm(dq_ref[0], wt_ref[:width]) + mm(dkv[rows], wt_ref[width:])
        dx_ref[0] = dx.astype(BF)
        gain_sum += jnp.sum(dx * x_ref[0].astype(F32), axis=0, keepdims=True)
    dag_ref[...] += gain_sum


def project_back(line, dkvs, dq, raw, xn, wt, cos, sin, k_gain):
    g, b, m = xn[0].shape
    c = wt.shape[0]
    width = dq[0].shape[2]
    heads = width // HEAD
    table = pl.BlockSpec((1, HALF, b), lambda g, i, at: (i, 0, 0))
    return line.call(
        functools.partial(project_back_kernel, len(dkvs)),
        *dkvs, *dq, raw, *xn, wt, cos, sin, k_gain,
        grid=(g, 2),
        in_specs=[per_block((1, b, 2 * HEAD))] * len(dkvs)
        + [per_block((1, b // 2, width))] * 2
        + [pl.BlockSpec((1, 1, HEAD, b), lambda g, i, at: (g, i, heads, 0))]
        + [per_block((1, b // 2, m))] * 2
        + [constant((c, m)), table, table, constant((HEAD, 1))],
        out_specs=[per_block((1, b // 2, m))] * 2
        + [per_block((1, b // 2, 2 * HEAD))] * 2
        + [constant((HEAD, b)), constant((1, m))],
        out_shape=[shape_of((g, b, m))] * 2
        + [shape_of((g, b, 2 * HEAD))] * 2
        + [shape_of((HEAD, b), F32), shape_of((1, m), F32)],
        cost=cost(4 * g * b * m * c, 8 * g * b * m + 2 * c * m + 16 * g * b * c),
        name="project_back",
    )


def ffn_kernel(
    tiles, at_ref, ha_ref, hb_ref, ga_ref, gb_ref, wg_ref, wu_ref, wd_ref, wgr_ref, wur_ref,
    db_ref, da_ref, act_ref, dgate_ref, dup_ref, keep_ref,
):
    t = pl.program_id(0)
    rows = ha_ref.shape[0]

    @pl.when(t < tiles)
    def _():
        for k, (h_ref, g_ref) in enumerate(((ha_ref, ga_ref), (hb_ref, gb_ref))):
            at = slice(k * rows, (k + 1) * rows)
            gate = mm(h_ref[...], wg_ref[...])
            up = mm(h_ref[...], wu_ref[...])
            dact = mm(g_ref[...], wd_ref[...], NT)
            sig = 1.0 / (1.0 + jnp.exp(-gate))
            silu = gate * sig
            act_ref[at, :] = (silu * up).astype(BF)
            dgate = (dact * up * (sig * (1.0 + gate * (1.0 - sig)))).astype(BF)
            dup = (dact * silu).astype(BF)
            dgate_ref[at, :] = dgate
            dup_ref[at, :] = dup
            keep_ref[t, 0, at, :] = dgate
            keep_ref[t, 1, at, :] = dup

    @pl.when(t >= tiles)
    def _():
        tile = keep_ref.shape[3]
        for k, d_ref in enumerate((da_ref, db_ref)):
            at = slice(k * rows, (k + 1) * rows)
            total = None
            for u in range(tiles):
                columns = slice(u * tile, (u + 1) * tile)
                part = mm(keep_ref[u, 0, at, :], wgr_ref[:, columns], NT)
                part += mm(keep_ref[u, 1, at, :], wur_ref[:, columns], NT)
                total = part if total is None else total + part
            d_ref[...] = total.astype(BF)


def ffn(line, hn, g, w_gate, w_up, w_down):
    r, m = hn[0].shape
    hidden = w_gate.shape[1] // 2
    tile, block = 256, 256
    tiles = hidden // tile

    def forward(t):
        return jnp.minimum(t, tiles - 1)

    def backward(t):
        return jnp.maximum(t - tiles, 0)

    columns = pl.BlockSpec((m, tile), lambda t, at: (0, at[2] * tiles + forward(t)))
    block_rows = pl.BlockSpec((block, hidden), lambda t, at: (backward(t), at[2]))
    d_block = pl.BlockSpec((r, block), lambda t, at: (0, backward(t)))
    hidden_block = pl.BlockSpec((2 * r, tile), lambda t, at: (0, forward(t)))
    return line.call(
        functools.partial(ffn_kernel, tiles), *hn, *g, w_gate, w_up, w_down, w_gate, w_up,
        grid=(tiles + m // block,),
        in_specs=[constant((r, m))] * 4
        + [
            columns,
            columns,
            pl.BlockSpec((tile, m), lambda t, at: (at[2] * tiles + forward(t), 0)),
            block_rows,
            block_rows,
        ],
        out_specs=[d_block, d_block, hidden_block, hidden_block, hidden_block],
        scratch=[pltpu.VMEM((tiles, 2, 2 * r, tile), BF)],
        out_shape=[shape_of((r, m))] * 2 + [shape_of((2 * r, hidden))] * 3,
        cost=cost(20 * r * m * hidden, 10 * m * hidden + 12 * r * m + 12 * r * hidden),
        name="ffn",
    )


def down_kernel(at_ref, act_ref, wd_ref, b_ref, a_ref):
    r = a_ref.shape[0]
    y = mm(act_ref[...], wd_ref[...]).astype(BF)
    a_ref[...] = y[:r]
    b_ref[...] = y[r:]


def down(line, act, w_down):
    rows, hidden = act.shape
    m = w_down.shape[1]
    block = 256
    out = pl.BlockSpec((rows // 2, block), lambda t, at: (0, t))
    return line.call(
        down_kernel, act, w_down,
        grid=(m // block,),
        in_specs=[
            constant((rows, hidden)),
            pl.BlockSpec((hidden, block), lambda t, at: (at[2], t)),
        ],
        out_specs=[out, out],
        out_shape=[shape_of((rows // 2, m))] * 2,
        cost=cost(2 * rows * hidden * m, 2 * (rows * hidden + hidden * m + rows * m)),
        name="down",
    )


def chip_sum_kernel(at_ref, a_ref, b_ref, *out_refs):
    share = out_refs[0].shape[1]
    for k, ref in enumerate(out_refs):
        at = slice(k * share, (k + 1) * share)
        ref[0] = (a_ref[0, at, :].astype(F32) + b_ref[0, at, :].astype(F32)).astype(BF)


def chip_sum(line, a, b):
    g, rows, m = a.shape
    return line.call(
        chip_sum_kernel, a, b,
        grid=(g,),
        in_specs=[per_sequence((1, rows, m))] * 2,
        out_specs=[per_sequence((1, rows // 4, m))] * 4,
        out_shape=[shape_of((g, rows // 4, m))] * 4,
        cost=cost(g * rows * m, 6 * g * rows * m),
        name="chip_sum",
    )


def stack_kernel(at_ref, *refs):
    share = refs[0].shape[1]
    for k, ref in enumerate(refs[:-1]):
        refs[-1][0, k * share : (k + 1) * share, :] = ref[0]


def stack(line, pieces):
    g, share, m = pieces[0].shape
    count = len(pieces)
    return line.call(
        stack_kernel, *pieces,
        grid=(g,),
        in_specs=[per_sequence((1, share, m))] * count,
        out_specs=per_sequence((1, count * share, m)),
        out_shape=shape_of((g, count * share, m)),
        cost=cost(0, 4 * g * count * share * m),
        name="stack",
    )


def mask_kernel(n_rows, share, at_ref, g_ref, out_ref):
    length = at_ref[3 + pl.program_id(0)]
    first = at_ref[0] * n_rows + at_ref[1] * share
    p = first + lax.broadcasted_iota(jnp.int32, (share, 1), 0)
    out_ref[0] = jnp.where(p < length, g_ref[0].astype(F32), 0.0).astype(BF)


def mask(line, grad, b):
    g, share, m = grad.shape
    return line.call(
        functools.partial(mask_kernel, b, share), grad,
        grid=(g,),
        in_specs=[per_sequence((1, share, m))],
        out_specs=per_sequence((1, share, m)),
        out_shape=shape_of((g, share, m)),
        cost=cost(g * share * m, 4 * g * share * m),
        name="mask",
    )


def middle_kernel(at_ref, own_ref, x_ref, z_ref, d_ref, tok_ref, gain_ref, hn_ref, h_ref):
    h = tok_ref[0].astype(F32)
    for ref in (own_ref, x_ref, z_ref, d_ref):
        h += ref[0].astype(F32)
    h_ref[0] = h
    r = lax.rsqrt(jnp.mean(h * h, axis=-1, keepdims=True) + EPS)
    hn_ref[0] = (h * r * gain_ref[...]).astype(BF)


def middle(line, pieces, tok, gain):
    g, share, m = tok.shape
    piece = per_sequence((1, share, m))
    return line.call(
        middle_kernel, *pieces, tok, gain,
        grid=(g,),
        in_specs=[piece] * 5 + [constant((1, m))],
        out_specs=[piece] * 2,
        out_shape=[shape_of((g, share, m)), shape_of((g, share, m), F32)],
        cost=cost(10 * g * share * m, 16 * g * share * m),
        name="middle",
    )


def middle_back_kernel(at_ref, own_ref, x_ref, z_ref, d_ref, h_ref, g_ref, gain_ref, low_ref, dh_ref, dg_ref):
    e = own_ref[0].astype(F32)
    for ref in (x_ref, z_ref, d_ref):
        e += ref[0].astype(F32)
    h = h_ref[0]
    r = lax.rsqrt(jnp.mean(h * h, axis=-1, keepdims=True) + EPS)
    unit = h * r
    ge = gain_ref[...] * e
    dh = g_ref[0].astype(F32) + r * (ge - unit * jnp.mean(ge * unit, axis=-1, keepdims=True))
    dh_ref[0] = dh
    low_ref[0] = dh.astype(BF)

    @pl.when(pl.program_id(0) == 0)
    def _():
        dg_ref[...] = jnp.zeros_like(dg_ref)

    dg_ref[...] += jnp.sum(e * unit, axis=0, keepdims=True)


def middle_back(line, pieces, h, grad, gain):
    g, share, m = h.shape
    piece = per_sequence((1, share, m))
    return line.call(
        middle_back_kernel, *pieces, h, grad, gain,
        grid=(g,),
        in_specs=[piece] * 6 + [constant((1, m))],
        out_specs=[piece, piece, constant((1, m))],
        out_shape=[shape_of((g, share, m)), shape_of((g, share, m), F32), shape_of((1, m), F32)],
        cost=cost(20 * g * share * m, 20 * g * share * m),
        name="middle_back",
    )


def grad_kernel(received, final, at_ref, la_ref, lb_ref, ra_ref, rb_ref, *refs):
    out_ref = refs[-1]

    def own():
        total = mm(la_ref[...], ra_ref[...], TN) + mm(lb_ref[...], rb_ref[...], TN)
        for ref in refs[:received]:
            total += ref[...].astype(F32)
        return total

    if final:

        @pl.when(pl.program_id(0) == 0)
        def _():
            out_ref[...] = own()

        @pl.when(pl.program_id(0) == 1)
        def _():
            out_ref[...] = refs[received][...].astype(F32)
    else:
        out_ref[...] = own().astype(BF)


def grad_stage(line, masks, left, right, received, peer=None):
    r, m = left[0].shape
    c = right[0][0].shape[1]
    count = lax.axis_size("narrow")
    block = m // count
    first, final = masks[0], peer is not None
    step = masks[1] - masks[0] if len(masks) > 1 else 0
    assert list(masks) == [first + k * step for k in range(len(masks))]

    def which(k):
        return 0 if final else k

    if block % 128:
        left = [jnp.moveaxis(x.reshape(r, count, block), 1, 0) for x in left]
        left_spec = pl.BlockSpec(
            (None, r, block), lambda k, at: (at[0] ^ (first + which(k) * step), 0, 0)
        )
    else:
        left_spec = pl.BlockSpec((r, block), lambda k, at: (0, at[0] ^ (first + which(k) * step)))
    arrays = [left[0], left[1], right[0][0], right[1][0]]
    specs = [left_spec, left_spec] + [
        pl.BlockSpec((r, c), lambda k, at, rows=rows: (rows, 0)) for _, rows in right
    ]
    for x, begin in received + ([(peer, 0)] if final else []):
        arrays.append(x)
        specs.append(
            pl.BlockSpec((None, block, c), lambda k, at, begin=begin: (begin + which(k), 0, 0))
        )
    if final:
        grid = (2,)
        out_spec = pl.BlockSpec((block, c), lambda k, at: (0, k ^ at[2]))
        out_shape = shape_of((block, 2 * c), F32)
    else:
        grid = (len(masks),)
        out_spec = pl.BlockSpec((None, block, c), lambda k, at: (k, 0, 0))
        out_shape = shape_of((len(masks), block, c))
    return line.call(
        functools.partial(grad_kernel, len(received), final), *arrays,
        grid=grid,
        in_specs=specs,
        out_specs=out_spec,
        out_shape=out_shape,
        cost=cost(
            4 * r * block * c * len(masks),
            4 * r * (block * len(masks) + c) + (2 + 2 * len(received)) * len(masks) * block * c,
        ),
        name="grad",
    )


def swap(x, narrow_mask, wide_mask):
    wide = lax.axis_size("wide")
    count = lax.axis_size("narrow") * wide
    mask = narrow_mask * wide + wide_mask
    return lax.ppermute(x, AXES, [(d, d ^ mask) for d in range(count)])


PEERS = ((0, 2), (TP_BIT, 0), (TP_BIT, 2))


def send(x):
    return [x] + [swap(x, *peer) for peer in PEERS]


def gathered(line, pieces):
    a = stack(line, pieces)
    return a, swap(a, 0, 1)


def scatter(line, a, b):
    pieces = chip_sum(line, a, b)
    return [pieces[0]] + [swap(piece, *peer) for piece, peer in zip(pieces[1:], PEERS)]


def added(pieces):
    return functools.reduce(lambda x, y: x + y, [p.astype(F32) for p in pieces])


def row_masks(count):
    return [(k & 1) | ((k >> 1) << 2) for k in range(count // 2)]


def add_kernel(at_ref, x_ref, y_ref, out_ref):
    out_ref[...] = x_ref[...] + y_ref[...]


class Total:
    def __init__(self, line, x):
        self.line, self.x = line, x
        narrow = [1 << k for k in range(lax.axis_size("narrow").bit_length() - 1)]
        wide = [1 << k for k in range(lax.axis_size("wide").bit_length() - 1)]
        self.steps = [(0, k) for k in wide] + [(TP_BIT, 0)] + [(k, 0) for k in narrow if k != TP_BIT]
        self.sent = swap(x, *self.steps.pop(0))

    def step(self):
        whole = constant(self.x.shape)
        self.x = self.line.call(
            add_kernel, self.x, self.sent,
            grid=(1,), in_specs=[whole, whole], out_specs=whole, out_shape=shape_of(self.x.shape, F32), name="add",
        )
        self.sent = swap(self.x, *self.steps.pop(0)) if self.steps else None

    def rest(self):
        while self.sent is not None:
            self.step()
        return self.x


class WeightGrad:
    def __init__(self, line, count, left, right):
        self.line, self.left, self.right = line, left, right
        self.masks = list(range(count))
        self.bits = [1] + [
            bit for k in range(1, count.bit_length()) if 1 < (bit := count >> k) < count and bit != TP_BIT
        ]
        self.received = []

    def step(self):
        bit = self.bits.pop(0)
        away = [k for k in self.masks if k & bit]
        begin = self.masks.index(away[0])
        self.masks = [k for k in self.masks if not k & bit]
        part = grad_stage(self.line, away, self.left, self.right, [(x, begin) for x in self.received])
        self.received.append(swap(part, bit, 0))

    def rest(self):
        while self.bits:
            self.step()

    def last(self):
        self.rest()
        part = grad_stage(self.line, [TP_BIT], self.left, self.right, [(x, 1) for x in self.received])
        self.peer = swap(part, TP_BIT, 0)

    def finish(self):
        received = [(x, 0) for x in self.received]
        return grad_stage(self.line, [0], self.left, self.right, received, self.peer)


def unit_rows(v):
    r = lax.rsqrt(jnp.mean(v * v, axis=-1, keepdims=True) + EPS)
    return v * r, r


def norm_back(unit, r, gain, grad):
    ge = gain * grad
    return r * (ge - unit * jnp.mean(ge * unit, axis=-1, keepdims=True))


def shards(
    tokens, lengths, attn_gain, w_query, key_matrix, value_matrix, q_gain, k_gain, w_out, ffn_gain,
    w_gate, w_up, w_down, out_grad,
):
    n, w = lax.axis_index("narrow"), lax.axis_index("wide")
    count = lax.axis_size("narrow")
    share, seqs, m = tokens.shape
    b = share * lax.axis_size("wide")
    half = (n // TP_BIT) % 2
    width = w_query.shape[1] // 2
    kv_width = key_matrix.shape[1] // 2

    def own_columns(x, size):
        return lax.dynamic_slice_in_dim(x, half * size, size, 1)

    wt = jnp.concatenate(
        [own_columns(w_query, width), own_columns(key_matrix, kv_width), own_columns(value_matrix, kv_width)],
        axis=1,
    ).T
    inside = position_inside(jnp.arange(b, dtype=jnp.int32), share, w)
    positions = jnp.stack([n * b + inside, (n ^ TP_BIT) * b + inside]).astype(F32)
    freqs = jnp.exp(-math.log(10000.0) * jnp.arange(HALF, dtype=F32) * 2.0 / HEAD)
    angles = positions[:, None, :] * freqs[None, :, None]
    cos, sin = jnp.cos(angles), jnp.sin(angles)
    qg, kg = q_gain[:, None], k_gain[:, None]
    line = Line(jnp.concatenate([jnp.stack([n, w, half]).astype(jnp.int32), lengths]))
    masks = row_masks(count)
    rows = seqs * b
    shape = (seqs, b, m)

    def flat(pair):
        return tuple(x.reshape(rows, x.shape[-1]) for x in pair)

    def whole(pair):
        return tuple((x, 0) for x in flat(pair))

    def halves(x):
        return ((x, 0), (x, 1))

    def weight(left, right):
        return WeightGrad(line, count, flat(left), right)

    tok = jnp.moveaxis(tokens, 1, 0)
    out_grad = jnp.moveaxis(out_grad, 1, 0)

    tok_unit, tok_r = unit_rows(tok.astype(F32))
    xn = gathered(line, send((tok_unit * attn_gain).astype(BF)))
    kv, q, raw = project(line, xn, wt, cos, sin, qg, kg)
    kvs = [swap(kv, k, 0) if k else kv for k in masks]
    grad = mask(line, out_grad, b)
    grad_pieces = send(grad)
    pb, pa, oa, ob, log = attend(line, q, kvs, w_out, share)
    pb = swap(pb, 0, 1)
    pieces = scatter(line, pa, pb)
    g_all = gathered(line, grad_pieces)
    hn, h = middle(line, pieces, tok, ffn_gain[None])
    hn = gathered(line, send(hn))

    db, da, act, dgate, dup = ffn(line, flat(hn), flat(g_all), w_gate, w_up, w_down)
    db = swap(db, 0, 1)
    d_down = weight(g_all, halves(act))
    d_gate, d_up = weight(hn, halves(dgate)), weight(hn, halves(dup))
    d_down.step()
    pieces = scatter(line, da.reshape(shape), db.reshape(shape))
    d_gate.step()
    dhl, dh, ffn_gain_grad = middle_back(line, pieces, h, grad, ffn_gain[None])
    pieces = send(dhl)
    yb, ya = down(line, act, w_down)
    yb = swap(yb, 0, 1)
    dhl = gathered(line, pieces)
    d_down.rest()

    back = attend_back(line, dhl, q, kvs, w_out, (oa, ob), log, raw, cos, sin, qg, share)
    dq, dkvs, dqg = back[:2], back[2:-1], back[-1]
    dkvs = [swap(x, k, 0) if k else x for x, k in zip(dkvs, masks)]
    d_gate.rest()
    d_up.step()
    dxb, dxa, dkva, dkvb, dkg, dag = project_back(line, dkvs, dq, raw, xn, wt, cos, sin, kg)
    dxb = swap(dxb, 0, 1)
    d_query = weight(xn, whole(dq))
    d_query.step()
    pieces = scatter(line, dxa, dxb)
    gains = jnp.concatenate(
        [dag[0] / attn_gain, ffn_gain_grad[0], jnp.sum(dqg, axis=1), jnp.sum(dkg, axis=1)]
    )
    gains = Total(line, gains.reshape(-1, 128))
    d_kv = weight(xn, whole((dkva, dkvb)))
    d_kv.step()
    gains.step()
    d_out = weight(dhl, whole((oa, ob)))
    d_out.step()
    gains.step()
    y_pieces = scatter(line, ya.reshape(shape), yb.reshape(shape))
    d_up.rest()
    gains.step()
    d_query.rest()
    d_down.last()
    d_kv.rest()
    d_out.rest()
    d_gate.last()
    dxn = added(pieces)
    d_tokens = dh + norm_back(tok_unit, tok_r, attn_gain, dxn)
    mixed = (h + added(y_pieces)).astype(BF)
    down_grad = d_down.finish()
    gate_grad = d_gate.finish()
    d_up.last()
    d_query.last()
    d_kv.last()
    d_out.last()
    gains.step()
    up_grad = d_up.finish()
    query_grad = d_query.finish()
    kv_grad = d_kv.finish()
    out_grad_t = d_out.finish()
    gains = gains.rest().reshape(-1)
    kv_grad = kv_grad.reshape(-1, 2, 2, kv_width)
    return (
        jnp.moveaxis(mixed, 0, 1),
        jnp.moveaxis(d_tokens, 0, 1),
        gains[:m],
        query_grad,
        kv_grad[:, :, 0].reshape(-1, 2 * kv_width),
        kv_grad[:, :, 1].reshape(-1, 2 * kv_width),
        gains[2 * m : 2 * m + HEAD],
        gains[2 * m + HEAD :],
        out_grad_t,
        gains[m : 2 * m],
        gate_grad,
        up_grad,
        down_grad,
    )


def solution(mesh):
    rows = P(AXES, None, None)
    columns = P(None, "wide")
    block = P("narrow", "wide")
    in_specs = (
        rows, P(), P(), columns, columns, columns, P(), P(), P("wide", None), P(), columns, columns,
        P("wide", None), rows,
    )
    out_specs = (
        rows, rows, P(), block, block, block, P(), P(), block, P(), block, block, block,
    )
    return jax.shard_map(shards, mesh=mesh, in_specs=in_specs, out_specs=out_specs, check_vma=False)
```

```python
import functools
import math

import jax
import jax.numpy as jnp
from jax import lax
from jax.experimental import pallas as pl
from jax.experimental.pallas import tpu as pltpu
from jax.sharding import PartitionSpec as P

QUERY_HEADS = 32
KEY_VALUE_HEADS = 8
HEAD = 64
HALF = HEAD // 2
GROUP = QUERY_HEADS // KEY_VALUE_HEADS
EPS = 1e-06
SCALE = HEAD ** (-0.5)
AXES = ("narrow", "wide")
TP_BIT = 2
BF = jnp.bfloat16
F32 = jnp.float32
MIB = 2**20
KERNEL_FLOPS = 5 * 10**9

NN = (((1,), (0,)), ((), ()))
NT = (((1,), (1,)), ((), ()))
TN = (((0,), (0,)), ((), ()))


def mm(a, b, dims=NN):
    return lax.dot_general(a, b, dims, preferred_element_type=F32)


class Line:
    def __init__(self, at):
        self.at = at
        self.last = []
        self.needed = []

    def wait(self, *arrays):
        self.needed += arrays

    def call(self, kernel, *args, grid, in_specs, out_specs, out_shape, scratch=(), name=None, limit=52 * 2**20):
        extra = [*self.last, *self.needed]
        self.needed = []

        def body(at_ref, *refs):
            kernel(at_ref, *refs[len(extra) :])

        outs = pl.pallas_call(
            body,
            grid_spec=pltpu.PrefetchScalarGridSpec(
                num_scalar_prefetch=1,
                grid=grid,
                in_specs=[pl.BlockSpec(memory_space=pl.ANY)] * len(extra) + list(in_specs),
                out_specs=out_specs,
                scratch_shapes=scratch,
            ),
            out_shape=out_shape,
            compiler_params=pltpu.CompilerParams(vmem_limit_bytes=limit),
            cost_estimate=pl.CostEstimate(flops=KERNEL_FLOPS, bytes_accessed=0, transcendentals=0),
            name=name,
        )(self.at, *extra, *args)
        self.last = [outs[0] if isinstance(outs, (list, tuple)) else outs]
        return outs

    def small(self, kernel, *args, out_shape, name):
        spec = pl.BlockSpec(memory_space=pltpu.VMEM)
        outs = jax.tree.map(lambda _: spec, out_shape)
        return self.call(
            kernel, *args,
            grid=(), in_specs=[spec] * len(args), out_specs=outs, out_shape=out_shape, limit=8 * MIB, name=name,
        )


def position_inside(t, share, w):
    u = t // share
    return (((u & 1) << 1) | ((u >> 1) ^ (w & 1))) * share + t % share


def block_of(n, mask, i):
    return ((n ^ mask) & ~TP_BIT) | (TP_BIT * i)


def join(ref):
    return jnp.concatenate([ref[0, 0], ref[1, 0]], axis=0)


def split(ref, value):
    share = ref.shape[2]
    ref[0, 0] = value[:share]
    ref[1, 0] = value[share:]


def positions_in_block(size, share, w, axis):
    shape = (size, 1) if axis == 0 else (1, size)
    return position_inside(lax.broadcasted_iota(jnp.int32, shape, axis), share, w)


def constant(shape):
    return pl.BlockSpec(shape, lambda *_: (0,) * len(shape))


def per_block(shape):
    return pl.BlockSpec(shape, lambda g, i, at: (g, i) + (0,) * (len(shape) - 2))


def chips(share, columns):
    return pl.BlockSpec((2, 1, share, columns), lambda g, i, at: (i, g, 0, 0))


def per_sequence(shape):
    return pl.BlockSpec(shape, lambda g, *_: (g,) + (0,) * (len(shape) - 1))


def shape_of(shape, dtype=BF):
    return jax.ShapeDtypeStruct(shape, dtype)


def project_kernel(at_ref, a_ref, b_ref, wt_ref, cos_ref, sin_ref, qg_ref, kg_ref, kv_ref, q_ref, raw_ref):
    x = jnp.concatenate([join(a_ref), join(b_ref)], axis=0)
    y = mm(wt_ref[...], x, NT)
    heads = y.shape[0] // HEAD - 2
    width = heads * HEAD
    raw_ref[0, 0] = y[: width + HEAD]
    c, s = cos_ref[0], sin_ref[0]

    def norm_rope(v, gain):
        r = lax.rsqrt(jnp.mean(v * v, axis=0, keepdims=True) + EPS)
        n = v * r * gain
        a, b = n[:HALF], n[HALF:]
        return a * c - b * s, b * c + a * s

    q = []
    for h in range(heads):
        a, b = norm_rope(y[h * HEAD : (h + 1) * HEAD], qg_ref[...])
        q.append(jnp.concatenate([a, b], axis=0) * SCALE)
    q_ref[0, 0] = jnp.concatenate(q, axis=1).astype(BF)
    a, b = norm_rope(y[width : width + HEAD], kg_ref[...])
    kv = jnp.concatenate([a, b, y[width + HEAD :]], axis=0)
    kv_ref[0] = kv.T.astype(BF)


def project(line, xn, wt, cos, sin, q_gain, k_gain):
    _, g, share, m = xn[0].shape
    b = 4 * share
    c = wt.shape[0]
    heads = c // HEAD - 2
    table = pl.BlockSpec((1, HALF, b), lambda g, i, at: (i, 0, 0))
    return line.call(
        project_kernel, *xn, wt, cos, sin, q_gain, k_gain,
        grid=(g, 2),
        in_specs=[chips(share, m)] * 2
        + [constant((c, m)), table, table, constant((HEAD, 1)), constant((HEAD, 1))],
        out_specs=[
            per_block((1, b, 2 * HEAD)),
            per_block((1, 1, HEAD, heads * b)),
            per_block((1, 1, (heads + 1) * HEAD, b)),
        ],
        out_shape=[
            shape_of((g, 2 * b, 2 * HEAD)),
            shape_of((g, 2, HEAD, heads * b)),
            shape_of((g, 2, (heads + 1) * HEAD, b), F32),
        ],
        name="project",
    )


def attend_kernel(masks, share, at_ref, q_ref, *refs):
    kv_refs = refs[: len(masks)]
    wo_ref, pb_ref, pa_ref, oa_ref, ob_ref, log_ref, acc_ref = refs[len(masks) :]
    n, w = at_ref[0], at_ref[1]
    length = at_ref[3 + pl.program_id(0)]
    b = kv_refs[0].shape[1] // 2
    heads = q_ref.shape[3] // b
    nq = block_of(n, 0, pl.program_id(1))
    bound = jnp.minimum(nq * b + positions_in_block(b, share, w, 1), length - 1)
    bound = jnp.concatenate([bound] * heads, axis=1)
    acc_ref[...] = jnp.zeros_like(acc_ref)
    inside = positions_in_block(b, share, w, 0)
    low = lax.broadcasted_iota(jnp.int32, (b, 2 * HEAD), 1) < HEAD

    for k, kv_ref in enumerate(kv_refs):
        for tp in range(2):
            nk = block_of(n, masks[k], tp)

            def add(masked):
                kv = kv_ref[0, tp * b : (tp + 1) * b, :]
                p = jnp.exp(mm(kv[:, :HEAD], q_ref[0, 0]))
                if masked:
                    p = jnp.where(nk * b + inside <= bound, p, 0.0)
                acc_ref[...] += mm(jnp.where(low, jnp.ones_like(kv), kv), p.astype(BF), TN)

            whole = (nk < nq) & ((nk + 1) * b <= length)
            pl.when(whole)(functools.partial(add, False))
            pl.when((nk <= nq) & (nk * b < length) & jnp.logical_not(whole))(functools.partial(add, True))

    total = acc_ref[:1, :]
    log_ref[0, 0] = jnp.log(total)
    o = acc_ref[HEAD:, :] / total
    o = jnp.concatenate([o[:, h * b : (h + 1) * b] for h in range(heads)], axis=0).T.astype(BF)
    split(oa_ref, o[: b // 2])
    split(ob_ref, o[b // 2 :])
    part = mm(o, wo_ref[...]).astype(BF)
    split(pa_ref, part[: b // 2])
    split(pb_ref, part[b // 2 :])


def attend(line, q, kvs, masks, w_out, share):
    g, b = q.shape[0], kvs[0].shape[1] // 2
    heads = q.shape[3] // b
    m = w_out.shape[1]
    width = heads * HEAD
    return line.call(
        functools.partial(attend_kernel, masks, share), q, *kvs, w_out,
        grid=(g, 2),
        in_specs=[per_block((1, 1, HEAD, heads * b))]
        + [per_sequence((1, 2 * b, 2 * HEAD))] * len(kvs)
        + [pl.BlockSpec((width, m), lambda g, i, at: (at[2], 0))],
        out_specs=[chips(share, m)] * 2
        + [chips(share, width)] * 2
        + [per_block((1, 1, 1, heads * b))],
        out_shape=[shape_of((4, g, share, m))] * 2
        + [shape_of((4, g, share, width))] * 2
        + [shape_of((g, 2, 1, heads * b), F32)],
        scratch=[pltpu.VMEM((2 * HEAD, heads * b), F32)],
        name="attend",
    )


def attend_back_kernel(masks, share, at_ref, dha_ref, dhb_ref, q_ref, *refs):
    count = len(masks)
    kv_refs, refs = refs[:count], refs[count:]
    wo_ref, oa_ref, ob_ref, log_ref, raw_ref, cos_ref, sin_ref, qg_ref, dqa_ref, dqb_ref = refs[:10]
    dkv_refs, dqg_ref = refs[10 : 10 + count], refs[10 + count]
    q_ext, do_ext, delta, dq_acc, dkv_acc = refs[11 + count :]
    n, w = at_ref[0], at_ref[1]
    at_g, i = pl.program_id(0), pl.program_id(1)
    length = at_ref[3 + at_g]
    b = kv_refs[0].shape[1] // 2
    heads = q_ref.shape[3] // b
    nq = block_of(n, 0, i)
    bound = jnp.minimum(nq * b + positions_in_block(b, share, w, 1), length - 1)
    bound = jnp.concatenate([bound] * heads, axis=1)
    inside = positions_in_block(b, share, w, 0)

    @pl.when(i == 0)
    def _():
        dkv_acc[...] = jnp.zeros_like(dkv_acc)

    @pl.when((i == 0) & (at_g == 0))
    def _():
        dqg_ref[...] = jnp.zeros_like(dqg_ref)

    dq_acc[...] = jnp.zeros_like(dq_acc)

    @pl.when(nq * b < length)
    def _():
        dh = jnp.concatenate([join(dha_ref), join(dhb_ref)], axis=0)
        do = mm(wo_ref[...], dh, NT).astype(BF).astype(F32)
        o = jnp.concatenate([join(oa_ref), join(ob_ref)], axis=0).astype(F32).T

        def heads_side_by_side(x):
            return jnp.concatenate([x[h * HEAD : (h + 1) * HEAD] for h in range(heads)], axis=1)

        do = heads_side_by_side(do)
        delta[...] = jnp.sum(do * heads_side_by_side(o), axis=0, keepdims=True)
        none = jnp.zeros((HEAD, heads * b), BF)
        do_ext[...] = jnp.concatenate([none, do.astype(BF)], axis=0)
        q_ext[...] = jnp.concatenate([q_ref[0, 0], none], axis=0)

    for k, kv_ref in enumerate(kv_refs):
        for tp in range(2):
            nk = block_of(n, masks[k], tp)

            def add(masked):
                kv = kv_ref[0, tp * b : (tp + 1) * b, :]
                p = jnp.exp(mm(kv, q_ext[...]) - log_ref[0, 0])
                if masked:
                    p = jnp.where(nk * b + inside <= bound, p, 0.0)
                ds = (p * (mm(kv, do_ext[...]) - delta[...])).astype(BF)
                dq_acc[...] += mm(kv, ds, TN)
                rows = slice((2 * k + tp) * b, (2 * k + tp + 1) * b)
                dkv_acc[rows, :] += mm(ds, q_ext[...], NT) + mm(p.astype(BF), do_ext[...], NT)

            whole = (nk < nq) & ((nk + 1) * b <= length)
            seen = (nk <= nq) & (nk * b < length) & (nq * b < length)
            pl.when(seen & whole)(functools.partial(add, False))
            pl.when(seen & jnp.logical_not(whole))(functools.partial(add, True))

    c, s = cos_ref[0], sin_ref[0]
    parts = []
    gain_sum = jnp.zeros((HEAD, b), F32)
    for h in range(heads):
        dq = dq_acc[:HEAD, h * b : (h + 1) * b] * SCALE
        e1, e2 = dq[:HALF], dq[HALF:]
        e = jnp.concatenate([e1 * c + e2 * s, e2 * c - e1 * s], axis=0)
        v = raw_ref[0, 0, h * HEAD : (h + 1) * HEAD, :]
        r = lax.rsqrt(jnp.mean(v * v, axis=0, keepdims=True) + EPS)
        unit = v * r
        ge = qg_ref[...] * e
        parts.append(r * (ge - unit * jnp.mean(ge * unit, axis=0, keepdims=True)))
        gain_sum += e * unit
    dq = jnp.concatenate(parts, axis=0).T.astype(BF)
    split(dqa_ref, dq[: b // 2])
    split(dqb_ref, dq[b // 2 :])
    dqg_ref[...] += gain_sum

    @pl.when(i == 1)
    def _():
        for k, ref in enumerate(dkv_refs):
            ref[0] = dkv_acc[2 * k * b : 2 * (k + 1) * b, :].astype(BF)


def attend_back(line, dh, q, kvs, masks, w_out, o, log, raw, cos, sin, q_gain, share):
    g, b = q.shape[0], kvs[0].shape[1] // 2
    heads = q.shape[3] // b
    m = w_out.shape[1]
    width = heads * HEAD
    half_rows = chips(share, width)
    table = pl.BlockSpec((1, HALF, b), lambda g, i, at: (i, 0, 0))
    return line.call(
        functools.partial(attend_back_kernel, masks, share),
        *dh, q, *kvs, w_out, *o, log, raw, cos, sin, q_gain,
        grid=(g, 2),
        in_specs=[chips(share, m)] * 2
        + [per_block((1, 1, HEAD, heads * b))]
        + [per_sequence((1, 2 * b, 2 * HEAD))] * len(kvs)
        + [
            pl.BlockSpec((width, m), lambda g, i, at: (at[2], 0)),
            half_rows,
            half_rows,
            per_block((1, 1, 1, heads * b)),
            per_block((1, 1, width, b)),
            table,
            table,
            constant((HEAD, 1)),
        ],
        out_specs=[half_rows, half_rows]
        + [per_sequence((1, 2 * b, 2 * HEAD))] * len(kvs)
        + [constant((HEAD, b))],
        scratch=[
            pltpu.VMEM((2 * HEAD, heads * b), BF),
            pltpu.VMEM((2 * HEAD, heads * b), BF),
            pltpu.VMEM((1, heads * b), F32),
            pltpu.VMEM((2 * HEAD, heads * b), F32),
            pltpu.VMEM((2 * b * len(kvs), 2 * HEAD), F32),
        ],
        out_shape=[shape_of((4, g, share, width))] * 2
        + [shape_of((g, 2 * b, 2 * HEAD))] * len(kvs)
        + [shape_of((HEAD, b), F32)],
        name="attend_back",
    )


def project_back_kernel(count, at_ref, *refs):
    dkv_refs = refs[:count]
    (
        dqa_ref, dqb_ref, raw_ref, xa_ref, xb_ref, wt_ref, cos_ref, sin_ref, kg_ref,
        dxb_ref, dxa_ref, dwa_ref, dwb_ref, dkg_ref, dag_ref,
    ) = refs[count:]

    @pl.when((pl.program_id(0) == 0) & (pl.program_id(1) == 0))
    def _():
        dkg_ref[...] = jnp.zeros_like(dkg_ref)
        dag_ref[...] = jnp.zeros_like(dag_ref)

    total = dkv_refs[0][0].astype(F32)
    for ref in dkv_refs[1:]:
        total += ref[0].astype(F32)
    t = total.T
    half = total.shape[0] // 2
    c, s = cos_ref[0], sin_ref[0]
    e1, e2 = t[:HALF], t[HALF:HEAD]
    e = jnp.concatenate([e1 * c + e2 * s, e2 * c - e1 * s], axis=0)
    v = raw_ref[0, 0]
    r = lax.rsqrt(jnp.mean(v * v, axis=0, keepdims=True) + EPS)
    unit = v * r
    ge = kg_ref[...] * e
    dk = r * (ge - unit * jnp.mean(ge * unit, axis=0, keepdims=True))
    dkg_ref[...] += e * unit
    dkv = jnp.concatenate([dk, t[HEAD:]], axis=0).T.astype(BF)
    width = dqa_ref.shape[3]
    gain_sum = jnp.zeros(dag_ref.shape, F32)
    for rows, dq_ref, x_ref, dx_ref, dw_ref in (
        (slice(0, half), dqa_ref, xa_ref, dxa_ref, dwa_ref),
        (slice(half, 2 * half), dqb_ref, xb_ref, dxb_ref, dwb_ref),
    ):
        dqkv = jnp.concatenate([join(dq_ref), dkv[rows]], axis=1)
        split(dw_ref, dqkv)
        dx = mm(dqkv, wt_ref[...])
        split(dx_ref, dx.astype(BF))
        gain_sum += jnp.sum(dx * join(x_ref).astype(F32), axis=0, keepdims=True)
    dag_ref[...] += gain_sum


def project_back(line, dkvs, dq, raw, xn, wt, cos, sin, k_gain):
    _, g, share, m = xn[0].shape
    b = 4 * share
    c = wt.shape[0]
    width = dq[0].shape[3]
    heads = width // HEAD
    table = pl.BlockSpec((1, HALF, b), lambda g, i, at: (i, 0, 0))
    return line.call(
        functools.partial(project_back_kernel, len(dkvs)),
        *dkvs, *dq, raw, *xn, wt, cos, sin, k_gain,
        grid=(g, 2),
        in_specs=[per_block((1, b, 2 * HEAD))] * len(dkvs)
        + [chips(share, width)] * 2
        + [pl.BlockSpec((1, 1, HEAD, b), lambda g, i, at: (g, i, heads, 0))]
        + [chips(share, m)] * 2
        + [constant((c, m)), table, table, constant((HEAD, 1))],
        out_specs=[chips(share, m)] * 2
        + [chips(share, c)] * 2
        + [constant((HEAD, b)), constant((1, m))],
        out_shape=[shape_of((4, g, share, m))] * 2
        + [shape_of((4, g, share, c))] * 2
        + [shape_of((HEAD, b), F32), shape_of((1, m), F32)],
        name="project_back",
    )


def ffn_kernel(
    tiles, at_ref, ha_ref, hb_ref, ga_ref, gb_ref, wg_ref, wu_ref, wd_ref, wgr_ref, wur_ref,
    db_ref, da_ref, act_ref, dgate_ref, dup_ref, keep_ref,
):
    t = pl.program_id(0)
    rows = ha_ref.shape[0]

    @pl.when(t < tiles)
    def _():
        for k, (h_ref, g_ref) in enumerate(((ha_ref, ga_ref), (hb_ref, gb_ref))):
            at = slice(k * rows, (k + 1) * rows)
            gate = mm(h_ref[...], wg_ref[...])
            up = mm(h_ref[...], wu_ref[...])
            dact = mm(g_ref[...], wd_ref[...], NT)
            sig = 1.0 / (1.0 + jnp.exp(-gate))
            silu = gate * sig
            act_ref[at, :] = (silu * up).astype(BF)
            dgate = (dact * up * (sig * (1.0 + gate * (1.0 - sig)))).astype(BF)
            dup = (dact * silu).astype(BF)
            dgate_ref[at, :] = dgate
            dup_ref[at, :] = dup
            keep_ref[t, 0, at, :] = dgate
            keep_ref[t, 1, at, :] = dup

    @pl.when(t >= tiles)
    def _():
        tile = keep_ref.shape[3]
        for k, d_ref in enumerate((da_ref, db_ref)):
            at = slice(k * rows, (k + 1) * rows)
            total = None
            for u in range(tiles):
                columns = slice(u * tile, (u + 1) * tile)
                part = mm(keep_ref[u, 0, at, :], wgr_ref[:, columns], NT)
                part += mm(keep_ref[u, 1, at, :], wur_ref[:, columns], NT)
                total = part if total is None else total + part
            d_ref[...] = total.astype(BF)


def ffn(line, hn, g, w_gate, w_up, w_down):
    r, m = hn[0].shape
    hidden = w_gate.shape[1] // 2
    tile, block = 256, 256
    tiles = hidden // tile

    def forward(t):
        return jnp.minimum(t, tiles - 1)

    def backward(t):
        return jnp.maximum(t - tiles, 0)

    columns = pl.BlockSpec((m, tile), lambda t, at: (0, at[2] * tiles + forward(t)))
    block_rows = pl.BlockSpec((block, hidden), lambda t, at: (backward(t), at[2]))
    d_block = pl.BlockSpec((r, block), lambda t, at: (0, backward(t)))
    hidden_block = pl.BlockSpec((2 * r, tile), lambda t, at: (0, forward(t)))
    return line.call(
        functools.partial(ffn_kernel, tiles), *hn, *g, w_gate, w_up, w_down, w_gate, w_up,
        grid=(tiles + m // block,),
        in_specs=[constant((r, m))] * 4
        + [
            columns,
            columns,
            pl.BlockSpec((tile, m), lambda t, at: (at[2] * tiles + forward(t), 0)),
            block_rows,
            block_rows,
        ],
        out_specs=[d_block, d_block, hidden_block, hidden_block, hidden_block],
        scratch=[pltpu.VMEM((tiles, 2, 2 * r, tile), BF)],
        out_shape=[shape_of((r, m))] * 2 + [shape_of((2 * r, hidden))] * 3,
        name="ffn",
        limit=52 * MIB,
    )


def down_kernel(at_ref, act_ref, wd_ref, b_ref, a_ref):
    r = a_ref.shape[0]
    y = mm(act_ref[...], wd_ref[...]).astype(BF)
    a_ref[...] = y[:r]
    b_ref[...] = y[r:]


def down(line, act, w_down):
    rows, hidden = act.shape
    m = w_down.shape[1]
    block = 256
    out = pl.BlockSpec((rows // 2, block), lambda t, at: (0, t))
    return line.call(
        down_kernel, act, w_down,
        grid=(m // block,),
        in_specs=[
            constant((rows, hidden)),
            pl.BlockSpec((hidden, block), lambda t, at: (at[2], t)),
        ],
        out_specs=[out, out],
        out_shape=[shape_of((rows // 2, m))] * 2,
        name="down",
    )


def chip_sum_kernel(at_ref, a_ref, b_ref, out_ref):
    rows = out_ref.shape[0]
    for k in range(0, rows, rows // 8):
        at = slice(k, k + rows // 8)
        out_ref[at] = (a_ref[at].astype(F32) + b_ref[at].astype(F32)).astype(BF)


def chip_sum(line, a, b):
    return line.small(chip_sum_kernel, a, b, out_shape=shape_of(a.shape), name="chip_sum")


def write_four(ref, g, value):
    for k in range(4):
        ref[k, g] = value


def sum_four(ref, g):
    total = ref[0, g].astype(F32)
    for k in range(1, 4):
        total += ref[k, g].astype(F32)
    return total


def mask_kernel(n_rows, at_ref, g_ref, out_ref):
    seqs, share, _ = g_ref.shape
    first = at_ref[0] * n_rows + at_ref[1] * share
    p = first + lax.broadcasted_iota(jnp.int32, (share, 1), 0)
    for g in range(seqs):
        write_four(out_ref, g, jnp.where(p < at_ref[3 + g], g_ref[g].astype(F32), 0.0).astype(BF))


def mask(line, grad, b):
    g, share, m = grad.shape
    return line.small(
        functools.partial(mask_kernel, b), grad, out_shape=shape_of((4, g, share, m)), name="mask"
    )


def middle_kernel(at_ref, parts_ref, tok_ref, gain_ref, hn_ref, h_ref):
    for g in range(tok_ref.shape[0]):
        h = tok_ref[g].astype(F32) + sum_four(parts_ref, g)
        h_ref[g] = h
        r = lax.rsqrt(jnp.mean(h * h, axis=-1, keepdims=True) + EPS)
        write_four(hn_ref, g, (h * r * gain_ref[...]).astype(BF))


def middle(line, parts, tok, gain):
    return line.small(
        middle_kernel, parts, tok, gain,
        out_shape=[shape_of(parts.shape), shape_of(tok.shape, F32)], name="middle",
    )


def middle_back_kernel(at_ref, parts_ref, h_ref, g_ref, gain_ref, low_ref, dh_ref, dg_ref):
    dg = jnp.zeros(dg_ref.shape, F32)
    for g in range(h_ref.shape[0]):
        e = sum_four(parts_ref, g)
        h = h_ref[g]
        r = lax.rsqrt(jnp.mean(h * h, axis=-1, keepdims=True) + EPS)
        unit = h * r
        ge = gain_ref[...] * e
        dh = g_ref[g].astype(F32) + r * (ge - unit * jnp.mean(ge * unit, axis=-1, keepdims=True))
        dh_ref[g] = dh
        write_four(low_ref, g, dh.astype(BF))
        dg += jnp.sum(e * unit, axis=0, keepdims=True)
    dg_ref[...] = dg


def middle_back(line, parts, h, grad, gain):
    return line.small(
        middle_back_kernel, parts, h, grad[0], gain,
        out_shape=[shape_of(parts.shape), shape_of(h.shape, F32), shape_of(gain.shape, F32)],
        name="middle_back",
    )


def finish_mixed_kernel(at_ref, parts_ref, h_ref, out_ref):
    for g in range(h_ref.shape[0]):
        out_ref[g] = (h_ref[g] + sum_four(parts_ref, g)).astype(BF)


def finish_mixed(line, parts, h):
    return line.small(
        finish_mixed_kernel, parts, h, out_shape=shape_of(h.shape), name="finish_mixed"
    )


def finish_tokens_kernel(at_ref, parts_ref, tok_ref, dh_ref, gain_ref, out_ref):
    for g in range(tok_ref.shape[0]):
        e = sum_four(parts_ref, g)
        v = tok_ref[g].astype(F32)
        r = lax.rsqrt(jnp.mean(v * v, axis=-1, keepdims=True) + EPS)
        unit = v * r
        ge = gain_ref[...] * e
        out_ref[g] = dh_ref[g] + r * (ge - unit * jnp.mean(ge * unit, axis=-1, keepdims=True))


def finish_tokens(line, parts, tok, dh, gain):
    return line.small(
        finish_tokens_kernel, parts, tok, dh, gain, out_shape=shape_of(dh.shape, F32), name="finish_tokens"
    )


def turn_kernel(at_ref, a_ref, b_ref, out_ref):
    rows = a_ref.shape[0]
    out_ref[:, :rows] = a_ref[...].astype(F32).T.astype(BF)
    out_ref[:, rows:] = b_ref[...].astype(F32).T.astype(BF)


def turn(line, pair):
    r, m = pair[0].shape
    block = 512
    columns = pl.BlockSpec((r, block), lambda k, at: (0, k))
    return line.call(
        turn_kernel, *pair,
        grid=(m // block,),
        in_specs=[columns, columns],
        out_specs=pl.BlockSpec((block, 2 * r), lambda k, at: (k, 0)),
        out_shape=shape_of((m, 2 * r)),
        name="turn",
    )


def both_rows(left_ref, ra_ref, rb_ref, at=slice(None)):
    rows = ra_ref.shape[0]
    return mm(left_ref[:, :rows], ra_ref[:, at]) + mm(left_ref[:, rows:], rb_ref[:, at])


def grad_kernel(start, begins, at_ref, left_ref, ra_ref, rb_ref, *refs):
    out_ref, acc_ref = refs[-2:]
    width = out_ref.shape[1]
    acc_ref[...] = both_rows(left_ref, ra_ref, rb_ref, slice(start, start + width))
    for begin, ref in zip(begins, refs):
        low, high = max(begin, start), min(begin + ref.shape[1], start + width)
        acc_ref[:, low - start : high - start] += ref[:, low - begin : high - begin].astype(F32)
    out_ref[...] = acc_ref[...].astype(BF)


def grad_whole_kernel(starts, final, at_ref, left_ref, ra_ref, rb_ref, *refs):
    out_ref, acc_ref = refs[-2:]

    def own():
        acc_ref[...] = both_rows(left_ref, ra_ref, rb_ref)
        for start, ref in zip(starts, refs):
            acc_ref[:, start : start + ref.shape[1]] += ref[...].astype(F32)
        out_ref[...] = acc_ref[...].astype(out_ref.dtype)

    if final:
        pl.when(pl.program_id(0) == 0)(own)

        @pl.when(pl.program_id(0) == 1)
        def _():
            out_ref[...] = refs[-3][...].astype(F32)
    else:
        own()


class WeightGrad:
    def __init__(self, line, left, right):
        self.line, self.left, self.right = line, left, right
        self.count = count = lax.axis_size("narrow")
        m, rows = left.shape
        self.r = rows // 2
        self.c = right[0][0].shape[1]
        self.block = m // count
        far = [bit for k in range(1, count.bit_length()) if (bit := count >> k) > TP_BIT]
        self.orders = {True: [1] + far, False: far + [1]}
        self.received = []

    def call(self, kernel, masks, extra, **kwargs):
        step = masks[1] - masks[0] if len(masks) > 1 else 0
        assert masks == [masks[0] + k * step for k in range(len(masks))]
        fixed = len(masks) == 1

        def which(k):
            return 0 if fixed else k

        arrays = [self.left, self.right[0][0], self.right[1][0]]
        specs = [
            pl.BlockSpec(
                (self.block, 2 * self.r), lambda k, at: (at[0] ^ (masks[0] + which(k) * step), 0)
            )
        ] + [pl.BlockSpec((self.r, self.c), lambda k, at, rows=rows: (rows, 0)) for _, rows in self.right]
        for array, begin, stride in extra:
            arrays.append(array)
            specs.append(
                pl.BlockSpec(
                    (None, self.block, array.shape[2]),
                    lambda k, at, begin=begin, stride=stride: (begin + which(k) * stride, 0, 0),
                )
            )
        return self.line.call(kernel, *arrays, in_specs=specs, name="grad", **kwargs)

    def send(self, stage, start=0, width=None, near_first=True):
        width = width or self.c
        order = self.orders[near_first]
        bit = order[stage]
        away = [k for k in range(self.count) if k & bit and not any(k & b for b in order[:stage])]
        extra, begins = [], []
        for masks, begin, size, array in self.received:
            if away[0] in masks and begin < start + width and start < begin + size:
                stride = masks.index(away[1]) - masks.index(away[0]) if len(away) > 1 else 0
                extra.append((array, masks.index(away[0]), stride))
                begins.append(begin)
        part = self.call(
            functools.partial(grad_kernel, start, begins), away, extra,
            grid=(len(away),),
            out_specs=pl.BlockSpec((None, self.block, width), lambda k, at: (k, 0, 0)),
            out_shape=shape_of((len(away), self.block, width)),
            scratch=[pltpu.VMEM((self.block, width), F32)],
        )
        got = swap(part, bit, 0)
        self.received.append(([k ^ bit for k in away], start, width, got))
        return got

    def rest(self, start=0, width=None):
        for stage in range(1, len(self.orders[True])):
            got = self.send(stage, start, width)
        return got

    def far(self, start=0, width=None):
        for stage in range(len(self.orders[False]) - 1):
            got = self.send(stage, start, width, False)
        return got

    def near(self, start=0, width=None):
        return self.send(len(self.orders[False]) - 1, start, width, False)

    def whole(self, mask, final, **kwargs):
        extra = [
            (array, masks.index(mask), 0)
            for masks, _, _, array in self.received
            if mask in masks
        ]
        starts = [begin for masks, begin, _, _ in self.received if mask in masks]
        if final:
            extra.append((self.peer, 0, 0))
        return self.call(
            functools.partial(grad_whole_kernel, starts, final), [mask], extra,
            scratch=[pltpu.VMEM((self.block, self.c), F32)], **kwargs,
        )

    def last(self):
        part = self.whole(
            TP_BIT, False,
            grid=(1,),
            out_specs=pl.BlockSpec((None, self.block, self.c), lambda k, at: (0, 0, 0)),
            out_shape=shape_of((1, self.block, self.c)),
        )
        self.peer = swap(part, TP_BIT, 0)

    def finish(self):
        return self.whole(
            0, True,
            grid=(2,),
            out_specs=pl.BlockSpec((self.block, self.c), lambda k, at: (0, k ^ at[2])),
            out_shape=shape_of((self.block, 2 * self.c), F32),
        )


def prepare_kernel(at_ref, q_ref, k_ref, v_ref, out_ref):
    width = k_ref.shape[1] // 2

    def own(ref):
        x = ref[...].astype(F32)
        return jnp.where(at_ref[2] == 0, x[:, :width], x[:, width:])

    x = jnp.concatenate([q_ref[...].astype(F32), own(k_ref), own(v_ref)], axis=1)
    out_ref[...] = x.T.astype(BF)


def prepare(line, w_query, w_key, w_value):
    m = w_query.shape[0]
    width, kv_width = w_query.shape[1] // 2, w_key.shape[1]
    rows = 512
    kv = pl.BlockSpec((rows, kv_width), lambda j, at: (j, 0))
    return line.call(
        prepare_kernel, w_query, w_key, w_value,
        grid=(m // rows,),
        in_specs=[pl.BlockSpec((rows, width), lambda j, at: (j, at[2])), kv, kv],
        out_specs=pl.BlockSpec((width + kv_width, rows), lambda j, at: (0, j)),
        out_shape=shape_of((width + kv_width, m)),
        name="prepare",
    )


def swap(x, narrow_mask, wide_mask):
    wide = lax.axis_size("wide")
    count = lax.axis_size("narrow") * wide
    mask = narrow_mask * wide + wide_mask
    return lax.ppermute(x, AXES, [(d, d ^ mask) for d in range(count)])


def chip_groups():
    wide = lax.axis_size("wide")
    count = lax.axis_size("narrow") * wide
    masks = (0, 2, TP_BIT * wide, TP_BIT * wide + 2)
    groups = sorted({tuple(sorted(d ^ mask for mask in masks)) for d in range(count)})
    return [list(group) for group in groups]


def exchange(x):
    return lax.all_to_all(x, AXES, 0, 0, tiled=True, axis_index_groups=chip_groups())


def gathered(x):
    a = exchange(x)
    return a, swap(a, 0, 1)


def scatter(line, a, b, shape):
    return exchange(chip_sum(line, a, b).reshape(shape))


def row_masks(count):
    return [(k & 1) | ((k >> 1) << 2) for k in range(count // 2)]


class Total:
    def __init__(self, x):
        self.x = x
        narrow = [1 << k for k in range(lax.axis_size("narrow").bit_length() - 1)]
        wide = [1 << k for k in range(lax.axis_size("wide").bit_length() - 1)]
        self.steps = [(0, k) for k in wide] + [(TP_BIT, 0)] + [(k, 0) for k in narrow if k != TP_BIT]

    def step(self, line):
        sent = swap(after(self.x, line.last[0]), *self.steps.pop(0))
        self.x = self.x + sent
        return sent

    def rest(self, line):
        while self.steps:
            self.step(line)
        return self.x


def after(x, *others):
    return lax.optimization_barrier((x, *others))[0]


def unit_rows(v):
    r = lax.rsqrt(jnp.mean(v * v, axis=-1, keepdims=True) + EPS)
    return v * r, r


def shards(
    tokens, lengths, attn_gain, w_query, key_matrix, value_matrix, q_gain, k_gain, w_out, ffn_gain,
    w_gate, w_up, w_down, out_grad,
):
    n, w = lax.axis_index("narrow"), lax.axis_index("wide")
    count = lax.axis_size("narrow")
    share, seqs, m = tokens.shape
    b = share * lax.axis_size("wide")
    half = (n // TP_BIT) % 2

    inside = position_inside(jnp.arange(b, dtype=jnp.int32), share, w)
    positions = jnp.stack([block_of(n, 0, i) * b + inside for i in range(2)]).astype(F32)
    freqs = jnp.exp(-math.log(10000.0) * jnp.arange(HALF, dtype=F32) * 2.0 / HEAD)
    angles = positions[:, None, :] * freqs[None, :, None]
    cos, sin = jnp.cos(angles), jnp.sin(angles)
    qg, kg = q_gain[:, None], k_gain[:, None]
    line = Line(jnp.concatenate([jnp.stack([n, w, half]).astype(jnp.int32), lengths]))
    masks = row_masks(count)
    rows = seqs * b
    shape = (4, seqs, share, m)

    def flat(pair):
        return tuple(x.reshape(rows, x.shape[-1]) for x in pair)

    def whole(pair):
        return tuple((x, 0) for x in flat(pair))

    def halves(x):
        return ((x, 0), (x, 1))

    tok = jnp.moveaxis(tokens, 1, 0)
    out_grad = jnp.moveaxis(out_grad, 1, 0)

    unit, _ = unit_rows(tok.astype(F32))
    sent = exchange(jnp.broadcast_to((unit * attn_gain).astype(BF)[None], shape))
    grad = mask(line, out_grad, b)
    wt = prepare(line, w_query, key_matrix, value_matrix)
    sent = after(sent, wt)
    xn = (sent, swap(sent, 0, 1))
    g_own = exchange(after(grad, sent))
    kv, q, raw = project(line, xn, wt, cos, sin, qg, kg)
    kvs = [swap(kv, k, 0) if k else kv for k in masks]
    xn_turned = turn(line, flat(xn))
    line.wait(g_own)
    pb, pa, oa, ob, log = attend(line, q, kvs, masks, w_out, share)
    pb = swap(pb, 0, 1)
    g_all = (g_own, swap(g_own, 0, 1))
    parts = scatter(line, *flat((pa, pb)), shape)
    g_turned = turn(line, flat(g_all))
    hn, h = middle(line, parts, tok, ffn_gain[None])
    hn = gathered(hn)

    db, da, act, dgate, dup = ffn(line, flat(hn), flat(g_all), w_gate, w_up, w_down)
    db = swap(db, 0, 1)
    c = act.shape[1]
    first, rest = (0, c // 4), (c // 4, 3 * c // 4)
    d_down = WeightGrad(line, g_turned, halves(act))
    d_down.send(0)
    parts = scatter(line, da, db, shape)
    hn_turned = turn(line, flat(hn))
    d_gate = WeightGrad(line, hn_turned, halves(dgate))
    d_up = WeightGrad(line, hn_turned, halves(dup))
    u_first = d_up.far(*first)
    g_first = d_gate.send(0, *first)
    g_rest = d_gate.send(0, *rest)
    dhl, dh, ffn_gain_grad = middle_back(line, parts, h, grad, ffn_gain[None])
    dhl = exchange(dhl)
    line.wait(u_first)
    d_first = d_down.rest(*first)
    yb, ya = down(line, act, w_down)
    yb = swap(yb, 0, 1)
    d_rest = d_down.rest(*rest)
    dhl = after(dhl, line.last[0], g_first, d_first, yb)
    dhl = (dhl, swap(dhl, 0, 1))
    mixed_parts = scatter(line, ya, yb, shape)

    back = attend_back(line, dhl, q, kvs, masks, w_out, (oa, ob), log, raw, cos, sin, qg, share)
    dq, dkvs, dqg = back[:2], after(tuple(back[2:-1]), g_rest, d_rest), back[-1]
    dkvs = [swap(x, k, 0) if k else x for x, k in zip(dkvs, masks)]
    dhl_turned = turn(line, flat(dhl))
    dxb, dxa, dwa, dwb, dkg, dag = project_back(line, dkvs, dq, raw, xn, wt, cos, sin, kg)
    dxb = swap(dxb, 0, 1)
    mixed = finish_mixed(line, mixed_parts, h)
    parts = scatter(line, *flat((dxa, dxb)), shape)
    g_z = d_gate.rest()
    d_qkv = WeightGrad(line, xn_turned, whole((dwa, dwb)))
    d_qkv.send(0)
    d_out = WeightGrad(line, dhl_turned, whole((oa, ob)))
    d_out.send(0)
    d_up.send(0, *rest)
    d_up.near(*first)
    gains = jnp.concatenate(
        [dag[0] / attn_gain, ffn_gain_grad[0], jnp.sum(dqg, axis=1), jnp.sum(dkg, axis=1)]
    )
    gains = Total(gains.reshape(-1, 128))
    sent = gains.step(line)
    d_down.last()
    line.wait(g_z, sent)
    d_tokens = finish_tokens(line, parts, tok, dh, attn_gain[None])
    sent = gains.step(line)
    d_qkv.rest()
    d_out.rest()
    u_z = d_up.rest(*rest)
    d_gate.last()
    down_grad = d_down.finish()
    line.wait(sent)
    d_qkv.last()
    sent = gains.step(line)
    gate_grad = d_gate.finish()
    line.wait(u_z)
    d_up.last()
    d_out.last()
    line.wait(sent)
    qkv_grad = d_qkv.finish()
    sent = gains.step(line)
    out_grad_t = d_out.finish()
    line.wait(sent)
    up_grad = d_up.finish()
    gains = gains.rest(line).reshape(-1)
    width = dq[0].shape[3]
    columns = dwa.shape[3]
    qkv_grad = qkv_grad.reshape(-1, 2, columns)
    query_grad = qkv_grad[:, :, :width].reshape(-1, 2 * width)
    return (
        jnp.moveaxis(mixed, 0, 1),
        jnp.moveaxis(d_tokens, 0, 1),
        gains[:m],
        query_grad,
        qkv_grad[:, :, width : width + HEAD].reshape(-1, 2 * HEAD),
        qkv_grad[:, :, width + HEAD :].reshape(-1, 2 * HEAD),
        gains[2 * m : 2 * m + HEAD],
        gains[2 * m + HEAD :],
        out_grad_t,
        gains[m : 2 * m],
        gate_grad,
        up_grad,
        down_grad,
    )


def solution(mesh):
    rows = P(AXES, None, None)
    columns = P(None, "wide")
    block = P("narrow", "wide")
    in_specs = (
        rows, P(), P(), columns, columns, columns, P(), P(), P("wide", None), P(), columns, columns,
        P("wide", None), rows,
    )
    out_specs = (
        rows, rows, P(), block, block, block, P(), P(), block, P(), block, block, block,
    )
    return jax.shard_map(shards, mesh=mesh, in_specs=in_specs, out_specs=out_specs, check_vma=False)
```

```python
import functools
import math

import jax
import jax.numpy as jnp
from jax import lax
from jax.experimental import pallas as pl
from jax.experimental.pallas import tpu as pltpu
from jax.sharding import PartitionSpec as P

QUERY_HEADS = 32
KEY_VALUE_HEADS = 8
HEAD = 64
HALF = HEAD // 2
GROUP = QUERY_HEADS // KEY_VALUE_HEADS
EPS = 1e-06
SCALE = HEAD ** (-0.5)
AXES = ("narrow", "wide")
TP_BIT = 2
BF = jnp.bfloat16
F32 = jnp.float32
MIB = 2**20
KERNEL_FLOPS = 5 * 10**9

NN = (((1,), (0,)), ((), ()))
NT = (((1,), (1,)), ((), ()))
TN = (((0,), (0,)), ((), ()))


def mm(a, b, dims=NN):
    return lax.dot_general(a, b, dims, preferred_element_type=F32)


class Line:
    def __init__(self, at):
        self.at = at
        self.last = []
        self.needed = []

    def wait(self, *arrays):
        self.needed += arrays

    def call(self, kernel, *args, grid, in_specs, out_specs, out_shape, scratch=(), name=None, limit=52 * 2**20):
        extra = [*self.last, *self.needed]
        self.needed = []

        def body(at_ref, *refs):
            kernel(at_ref, *refs[len(extra) :])

        outs = pl.pallas_call(
            body,
            grid_spec=pltpu.PrefetchScalarGridSpec(
                num_scalar_prefetch=1,
                grid=grid,
                in_specs=[pl.BlockSpec(memory_space=pl.ANY)] * len(extra) + list(in_specs),
                out_specs=out_specs,
                scratch_shapes=scratch,
            ),
            out_shape=out_shape,
            compiler_params=pltpu.CompilerParams(vmem_limit_bytes=limit),
            cost_estimate=pl.CostEstimate(flops=KERNEL_FLOPS, bytes_accessed=0, transcendentals=0),
            name=name,
        )(self.at, *extra, *args)
        self.last = [outs[0] if isinstance(outs, (list, tuple)) else outs]
        return outs

    def small(self, kernel, *args, out_shape, name):
        spec = pl.BlockSpec(memory_space=pltpu.VMEM)
        outs = jax.tree.map(lambda _: spec, out_shape)
        return self.call(
            kernel, *args,
            grid=(), in_specs=[spec] * len(args), out_specs=outs, out_shape=out_shape, limit=8 * MIB, name=name,
        )


def position_inside(t, share, w):
    u = t // share
    return (((u & 1) << 1) | ((u >> 1) ^ (w & 1))) * share + t % share


def block_of(n, mask, i):
    return ((n ^ mask) & ~TP_BIT) | (TP_BIT * i)


def join(ref):
    return jnp.concatenate([ref[0, 0], ref[1, 0]], axis=0)


def split(ref, value):
    share = ref.shape[2]
    ref[0, 0] = value[:share]
    ref[1, 0] = value[share:]


def positions_in_block(size, share, w, axis):
    shape = (size, 1) if axis == 0 else (1, size)
    return position_inside(lax.broadcasted_iota(jnp.int32, shape, axis), share, w)


def constant(shape):
    return pl.BlockSpec(shape, lambda *_: (0,) * len(shape))


def per_block(shape):
    return pl.BlockSpec(shape, lambda g, i, at: (g, i) + (0,) * (len(shape) - 2))


def chips(share, columns):
    return pl.BlockSpec((2, 1, share, columns), lambda g, i, at: (i, g, 0, 0))


def per_sequence(shape):
    return pl.BlockSpec(shape, lambda g, *_: (g,) + (0,) * (len(shape) - 1))


def shape_of(shape, dtype=BF):
    return jax.ShapeDtypeStruct(shape, dtype)


def project_kernel(at_ref, a_ref, b_ref, wt_ref, cos_ref, sin_ref, qg_ref, kg_ref, kv_ref, q_ref, raw_ref):
    x = jnp.concatenate([join(a_ref), join(b_ref)], axis=0)
    y = mm(wt_ref[...], x, NT)
    heads = y.shape[0] // HEAD - 2
    width = heads * HEAD
    raw_ref[0, 0] = y[: width + HEAD]
    c, s = cos_ref[0], sin_ref[0]

    def norm_rope(v, gain):
        r = lax.rsqrt(jnp.mean(v * v, axis=0, keepdims=True) + EPS)
        n = v * r * gain
        a, b = n[:HALF], n[HALF:]
        return a * c - b * s, b * c + a * s

    q = []
    for h in range(heads):
        a, b = norm_rope(y[h * HEAD : (h + 1) * HEAD], qg_ref[...])
        q.append(jnp.concatenate([a, b], axis=0) * SCALE)
    q_ref[0, 0] = jnp.concatenate(q, axis=1).astype(BF)
    a, b = norm_rope(y[width : width + HEAD], kg_ref[...])
    kv = jnp.concatenate([a, b, y[width + HEAD :]], axis=0)
    kv_ref[0] = kv.T.astype(BF)


def project(line, xn, wt, cos, sin, q_gain, k_gain):
    _, g, share, m = xn[0].shape
    b = 4 * share
    c = wt.shape[0]
    heads = c // HEAD - 2
    table = pl.BlockSpec((1, HALF, b), lambda g, i, at: (i, 0, 0))
    return line.call(
        project_kernel, *xn, wt, cos, sin, q_gain, k_gain,
        grid=(g, 2),
        in_specs=[chips(share, m)] * 2
        + [constant((c, m)), table, table, constant((HEAD, 1)), constant((HEAD, 1))],
        out_specs=[
            per_block((1, b, 2 * HEAD)),
            per_block((1, 1, HEAD, heads * b)),
            per_block((1, 1, (heads + 1) * HEAD, b)),
        ],
        out_shape=[
            shape_of((g, 2 * b, 2 * HEAD)),
            shape_of((g, 2, HEAD, heads * b)),
            shape_of((g, 2, (heads + 1) * HEAD, b), F32),
        ],
        name="project",
    )


def attend_kernel(masks, share, at_ref, q_ref, *refs):
    kv_refs = refs[: len(masks)]
    wo_ref, pb_ref, pa_ref, oa_ref, ob_ref, log_ref, acc_ref = refs[len(masks) :]
    n, w = at_ref[0], at_ref[1]
    length = at_ref[3 + pl.program_id(0)]
    b = kv_refs[0].shape[1] // 2
    heads = q_ref.shape[3] // b
    nq = block_of(n, 0, pl.program_id(1))
    bound = jnp.minimum(nq * b + positions_in_block(b, share, w, 1), length - 1)
    bound = jnp.concatenate([bound] * heads, axis=1)
    acc_ref[...] = jnp.zeros_like(acc_ref)
    inside = positions_in_block(b, share, w, 0)
    low = lax.broadcasted_iota(jnp.int32, (b, 2 * HEAD), 1) < HEAD

    for k, kv_ref in enumerate(kv_refs):
        for tp in range(2):
            nk = block_of(n, masks[k], tp)

            def add(masked):
                kv = kv_ref[0, tp * b : (tp + 1) * b, :]
                p = jnp.exp(mm(kv[:, :HEAD], q_ref[0, 0]))
                if masked:
                    p = jnp.where(nk * b + inside <= bound, p, 0.0)
                acc_ref[...] += mm(jnp.where(low, jnp.ones_like(kv), kv), p.astype(BF), TN)

            whole = (nk < nq) & ((nk + 1) * b <= length)
            pl.when(whole)(functools.partial(add, False))
            pl.when((nk <= nq) & (nk * b < length) & jnp.logical_not(whole))(functools.partial(add, True))

    total = acc_ref[:1, :]
    log_ref[0, 0] = jnp.log(total)
    o = acc_ref[HEAD:, :] / total
    o = jnp.concatenate([o[:, h * b : (h + 1) * b] for h in range(heads)], axis=0).T.astype(BF)
    split(oa_ref, o[: b // 2])
    split(ob_ref, o[b // 2 :])
    part = mm(o, wo_ref[...]).astype(BF)
    split(pa_ref, part[: b // 2])
    split(pb_ref, part[b // 2 :])


def attend(line, q, kvs, masks, w_out, share):
    g, b = q.shape[0], kvs[0].shape[1] // 2
    heads = q.shape[3] // b
    m = w_out.shape[1]
    width = heads * HEAD
    return line.call(
        functools.partial(attend_kernel, masks, share), q, *kvs, w_out,
        grid=(g, 2),
        in_specs=[per_block((1, 1, HEAD, heads * b))]
        + [per_sequence((1, 2 * b, 2 * HEAD))] * len(kvs)
        + [pl.BlockSpec((width, m), lambda g, i, at: (at[2], 0))],
        out_specs=[chips(share, m)] * 2
        + [chips(share, width)] * 2
        + [per_block((1, 1, 1, heads * b))],
        out_shape=[shape_of((4, g, share, m))] * 2
        + [shape_of((4, g, share, width))] * 2
        + [shape_of((g, 2, 1, heads * b), F32)],
        scratch=[pltpu.VMEM((2 * HEAD, heads * b), F32)],
        name="attend",
    )


def attend_back_kernel(masks, share, at_ref, dha_ref, dhb_ref, q_ref, *refs):
    count = len(masks)
    kv_refs, refs = refs[:count], refs[count:]
    wo_ref, oa_ref, ob_ref, log_ref, raw_ref, cos_ref, sin_ref, qg_ref, dqa_ref, dqb_ref = refs[:10]
    dkv_refs, dqg_ref = refs[10 : 10 + count], refs[10 + count]
    q_ext, do_ext, delta, dq_acc, dkv_acc = refs[11 + count :]
    n, w = at_ref[0], at_ref[1]
    at_g, i = pl.program_id(0), pl.program_id(1)
    length = at_ref[3 + at_g]
    b = kv_refs[0].shape[1] // 2
    heads = q_ref.shape[3] // b
    nq = block_of(n, 0, i)
    bound = jnp.minimum(nq * b + positions_in_block(b, share, w, 1), length - 1)
    bound = jnp.concatenate([bound] * heads, axis=1)
    inside = positions_in_block(b, share, w, 0)

    @pl.when(i == 0)
    def _():
        dkv_acc[...] = jnp.zeros_like(dkv_acc)

    @pl.when((i == 0) & (at_g == 0))
    def _():
        dqg_ref[...] = jnp.zeros_like(dqg_ref)

    dq_acc[...] = jnp.zeros_like(dq_acc)

    @pl.when(nq * b < length)
    def _():
        dh = jnp.concatenate([join(dha_ref), join(dhb_ref)], axis=0)
        do = mm(wo_ref[...], dh, NT).astype(BF).astype(F32)
        o = jnp.concatenate([join(oa_ref), join(ob_ref)], axis=0).astype(F32).T

        def heads_side_by_side(x):
            return jnp.concatenate([x[h * HEAD : (h + 1) * HEAD] for h in range(heads)], axis=1)

        do = heads_side_by_side(do)
        delta[...] = jnp.sum(do * heads_side_by_side(o), axis=0, keepdims=True)
        none = jnp.zeros((HEAD, heads * b), BF)
        do_ext[...] = jnp.concatenate([none, do.astype(BF)], axis=0)
        q_ext[...] = jnp.concatenate([q_ref[0, 0], none], axis=0)

    for k, kv_ref in enumerate(kv_refs):
        for tp in range(2):
            nk = block_of(n, masks[k], tp)

            def add(masked):
                kv = kv_ref[0, tp * b : (tp + 1) * b, :]
                p = jnp.exp(mm(kv, q_ext[...]) - log_ref[0, 0])
                if masked:
                    p = jnp.where(nk * b + inside <= bound, p, 0.0)
                ds = (p * (mm(kv, do_ext[...]) - delta[...])).astype(BF)
                dq_acc[...] += mm(kv, ds, TN)
                rows = slice((2 * k + tp) * b, (2 * k + tp + 1) * b)
                dkv_acc[rows, :] += mm(ds, q_ext[...], NT) + mm(p.astype(BF), do_ext[...], NT)

            whole = (nk < nq) & ((nk + 1) * b <= length)
            seen = (nk <= nq) & (nk * b < length) & (nq * b < length)
            pl.when(seen & whole)(functools.partial(add, False))
            pl.when(seen & jnp.logical_not(whole))(functools.partial(add, True))

    c, s = cos_ref[0], sin_ref[0]
    parts = []
    gain_sum = jnp.zeros((HEAD, b), F32)
    for h in range(heads):
        dq = dq_acc[:HEAD, h * b : (h + 1) * b] * SCALE
        e1, e2 = dq[:HALF], dq[HALF:]
        e = jnp.concatenate([e1 * c + e2 * s, e2 * c - e1 * s], axis=0)
        v = raw_ref[0, 0, h * HEAD : (h + 1) * HEAD, :]
        r = lax.rsqrt(jnp.mean(v * v, axis=0, keepdims=True) + EPS)
        unit = v * r
        ge = qg_ref[...] * e
        parts.append(r * (ge - unit * jnp.mean(ge * unit, axis=0, keepdims=True)))
        gain_sum += e * unit
    dq = jnp.concatenate(parts, axis=0).T.astype(BF)
    split(dqa_ref, dq[: b // 2])
    split(dqb_ref, dq[b // 2 :])
    dqg_ref[...] += gain_sum

    @pl.when(i == 1)
    def _():
        for k, ref in enumerate(dkv_refs):
            ref[0] = dkv_acc[2 * k * b : 2 * (k + 1) * b, :].astype(BF)


def attend_back(line, dh, q, kvs, masks, w_out, o, log, raw, cos, sin, q_gain, share):
    g, b = q.shape[0], kvs[0].shape[1] // 2
    heads = q.shape[3] // b
    m = w_out.shape[1]
    width = heads * HEAD
    half_rows = chips(share, width)
    table = pl.BlockSpec((1, HALF, b), lambda g, i, at: (i, 0, 0))
    return line.call(
        functools.partial(attend_back_kernel, masks, share),
        *dh, q, *kvs, w_out, *o, log, raw, cos, sin, q_gain,
        grid=(g, 2),
        in_specs=[chips(share, m)] * 2
        + [per_block((1, 1, HEAD, heads * b))]
        + [per_sequence((1, 2 * b, 2 * HEAD))] * len(kvs)
        + [
            pl.BlockSpec((width, m), lambda g, i, at: (at[2], 0)),
            half_rows,
            half_rows,
            per_block((1, 1, 1, heads * b)),
            per_block((1, 1, width, b)),
            table,
            table,
            constant((HEAD, 1)),
        ],
        out_specs=[half_rows, half_rows]
        + [per_sequence((1, 2 * b, 2 * HEAD))] * len(kvs)
        + [constant((HEAD, b))],
        scratch=[
            pltpu.VMEM((2 * HEAD, heads * b), BF),
            pltpu.VMEM((2 * HEAD, heads * b), BF),
            pltpu.VMEM((1, heads * b), F32),
            pltpu.VMEM((2 * HEAD, heads * b), F32),
            pltpu.VMEM((2 * b * len(kvs), 2 * HEAD), F32),
        ],
        out_shape=[shape_of((4, g, share, width))] * 2
        + [shape_of((g, 2 * b, 2 * HEAD))] * len(kvs)
        + [shape_of((HEAD, b), F32)],
        name="attend_back",
    )


def project_back_kernel(count, at_ref, *refs):
    dkv_refs = refs[:count]
    (
        dqa_ref, dqb_ref, raw_ref, xa_ref, xb_ref, wt_ref, cos_ref, sin_ref, kg_ref,
        dxb_ref, dxa_ref, dwa_ref, dwb_ref, dkg_ref, dag_ref,
    ) = refs[count:]

    @pl.when((pl.program_id(0) == 0) & (pl.program_id(1) == 0))
    def _():
        dkg_ref[...] = jnp.zeros_like(dkg_ref)
        dag_ref[...] = jnp.zeros_like(dag_ref)

    total = dkv_refs[0][0].astype(F32)
    for ref in dkv_refs[1:]:
        total += ref[0].astype(F32)
    t = total.T
    half = total.shape[0] // 2
    c, s = cos_ref[0], sin_ref[0]
    e1, e2 = t[:HALF], t[HALF:HEAD]
    e = jnp.concatenate([e1 * c + e2 * s, e2 * c - e1 * s], axis=0)
    v = raw_ref[0, 0]
    r = lax.rsqrt(jnp.mean(v * v, axis=0, keepdims=True) + EPS)
    unit = v * r
    ge = kg_ref[...] * e
    dk = r * (ge - unit * jnp.mean(ge * unit, axis=0, keepdims=True))
    dkg_ref[...] += e * unit
    dkv = jnp.concatenate([dk, t[HEAD:]], axis=0).T.astype(BF)
    width = dqa_ref.shape[3]
    gain_sum = jnp.zeros(dag_ref.shape, F32)
    for rows, dq_ref, x_ref, dx_ref, dw_ref in (
        (slice(0, half), dqa_ref, xa_ref, dxa_ref, dwa_ref),
        (slice(half, 2 * half), dqb_ref, xb_ref, dxb_ref, dwb_ref),
    ):
        dqkv = jnp.concatenate([join(dq_ref), dkv[rows]], axis=1)
        split(dw_ref, dqkv)
        dx = mm(dqkv, wt_ref[...])
        split(dx_ref, dx.astype(BF))
        gain_sum += jnp.sum(dx * join(x_ref).astype(F32), axis=0, keepdims=True)
    dag_ref[...] += gain_sum


def project_back(line, dkvs, dq, raw, xn, wt, cos, sin, k_gain):
    _, g, share, m = xn[0].shape
    b = 4 * share
    c = wt.shape[0]
    width = dq[0].shape[3]
    heads = width // HEAD
    table = pl.BlockSpec((1, HALF, b), lambda g, i, at: (i, 0, 0))
    return line.call(
        functools.partial(project_back_kernel, len(dkvs)),
        *dkvs, *dq, raw, *xn, wt, cos, sin, k_gain,
        grid=(g, 2),
        in_specs=[per_block((1, b, 2 * HEAD))] * len(dkvs)
        + [chips(share, width)] * 2
        + [pl.BlockSpec((1, 1, HEAD, b), lambda g, i, at: (g, i, heads, 0))]
        + [chips(share, m)] * 2
        + [constant((c, m)), table, table, constant((HEAD, 1))],
        out_specs=[chips(share, m)] * 2
        + [chips(share, c)] * 2
        + [constant((HEAD, b)), constant((1, m))],
        out_shape=[shape_of((4, g, share, m))] * 2
        + [shape_of((4, g, share, c))] * 2
        + [shape_of((HEAD, b), F32), shape_of((1, m), F32)],
        name="project_back",
    )


def ffn_kernel(
    tiles, at_ref, ha_ref, hb_ref, ga_ref, gb_ref, wg_ref, wu_ref, wd_ref, wgr_ref, wur_ref,
    db_ref, da_ref, act_ref, dgate_ref, dup_ref, keep_ref,
):
    t = pl.program_id(0)
    rows = ha_ref.shape[0]

    @pl.when(t < tiles)
    def _():
        for k, (h_ref, g_ref) in enumerate(((ha_ref, ga_ref), (hb_ref, gb_ref))):
            at = slice(k * rows, (k + 1) * rows)
            gate = mm(h_ref[...], wg_ref[...])
            up = mm(h_ref[...], wu_ref[...])
            dact = mm(g_ref[...], wd_ref[...], NT)
            sig = 1.0 / (1.0 + jnp.exp(-gate))
            silu = gate * sig
            act_ref[at, :] = (silu * up).astype(BF)
            dgate = (dact * up * (sig * (1.0 + gate * (1.0 - sig)))).astype(BF)
            dup = (dact * silu).astype(BF)
            dgate_ref[at, :] = dgate
            dup_ref[at, :] = dup
            keep_ref[t, 0, at, :] = dgate
            keep_ref[t, 1, at, :] = dup

    @pl.when(t >= tiles)
    def _():
        tile = keep_ref.shape[3]
        for k, d_ref in enumerate((da_ref, db_ref)):
            at = slice(k * rows, (k + 1) * rows)
            total = None
            for u in range(tiles):
                columns = slice(u * tile, (u + 1) * tile)
                part = mm(keep_ref[u, 0, at, :], wgr_ref[:, columns], NT)
                part += mm(keep_ref[u, 1, at, :], wur_ref[:, columns], NT)
                total = part if total is None else total + part
            d_ref[...] = total.astype(BF)


def ffn(line, hn, g, w_gate, w_up, w_down):
    r, m = hn[0].shape
    hidden = w_gate.shape[1] // 2
    tile, block = 256, 256
    tiles = hidden // tile

    def forward(t):
        return jnp.minimum(t, tiles - 1)

    def backward(t):
        return jnp.maximum(t - tiles, 0)

    columns = pl.BlockSpec((m, tile), lambda t, at: (0, at[2] * tiles + forward(t)))
    block_rows = pl.BlockSpec((block, hidden), lambda t, at: (backward(t), at[2]))
    d_block = pl.BlockSpec((r, block), lambda t, at: (0, backward(t)))
    hidden_block = pl.BlockSpec((2 * r, tile), lambda t, at: (0, forward(t)))
    return line.call(
        functools.partial(ffn_kernel, tiles), *hn, *g, w_gate, w_up, w_down, w_gate, w_up,
        grid=(tiles + m // block,),
        in_specs=[constant((r, m))] * 4
        + [
            columns,
            columns,
            pl.BlockSpec((tile, m), lambda t, at: (at[2] * tiles + forward(t), 0)),
            block_rows,
            block_rows,
        ],
        out_specs=[d_block, d_block, hidden_block, hidden_block, hidden_block],
        scratch=[pltpu.VMEM((tiles, 2, 2 * r, tile), BF)],
        out_shape=[shape_of((r, m))] * 2 + [shape_of((2 * r, hidden))] * 3,
        name="ffn",
        limit=52 * MIB,
    )


def down_kernel(at_ref, act_ref, wd_ref, b_ref, a_ref):
    r = a_ref.shape[0]
    y = mm(act_ref[...], wd_ref[...]).astype(BF)
    a_ref[...] = y[:r]
    b_ref[...] = y[r:]


def down(line, act, w_down):
    rows, hidden = act.shape
    m = w_down.shape[1]
    block = 256
    out = pl.BlockSpec((rows // 2, block), lambda t, at: (0, t))
    return line.call(
        down_kernel, act, w_down,
        grid=(m // block,),
        in_specs=[
            constant((rows, hidden)),
            pl.BlockSpec((hidden, block), lambda t, at: (at[2], t)),
        ],
        out_specs=[out, out],
        out_shape=[shape_of((rows // 2, m))] * 2,
        name="down",
    )


def chip_sum_kernel(at_ref, a_ref, b_ref, out_ref):
    rows = out_ref.shape[0]
    for k in range(0, rows, rows // 8):
        at = slice(k, k + rows // 8)
        out_ref[at] = (a_ref[at].astype(F32) + b_ref[at].astype(F32)).astype(BF)


def chip_sum(line, a, b):
    return line.small(chip_sum_kernel, a, b, out_shape=shape_of(a.shape), name="chip_sum")


def write_four(ref, g, value):
    for k in range(4):
        ref[k, g] = value


def sum_four(ref, g):
    total = ref[0, g].astype(F32)
    for k in range(1, 4):
        total += ref[k, g].astype(F32)
    return total


def mask_kernel(n_rows, at_ref, g_ref, out_ref):
    seqs, share, _ = g_ref.shape
    first = at_ref[0] * n_rows + at_ref[1] * share
    p = first + lax.broadcasted_iota(jnp.int32, (share, 1), 0)
    for g in range(seqs):
        write_four(out_ref, g, jnp.where(p < at_ref[3 + g], g_ref[g].astype(F32), 0.0).astype(BF))


def mask(line, grad, b):
    g, share, m = grad.shape
    return line.small(
        functools.partial(mask_kernel, b), grad, out_shape=shape_of((4, g, share, m)), name="mask"
    )


def middle_kernel(at_ref, parts_ref, tok_ref, gain_ref, hn_ref, h_ref):
    for g in range(tok_ref.shape[0]):
        h = tok_ref[g].astype(F32) + sum_four(parts_ref, g)
        h_ref[g] = h
        r = lax.rsqrt(jnp.mean(h * h, axis=-1, keepdims=True) + EPS)
        write_four(hn_ref, g, (h * r * gain_ref[...]).astype(BF))


def middle(line, parts, tok, gain):
    return line.small(
        middle_kernel, parts, tok, gain,
        out_shape=[shape_of(parts.shape), shape_of(tok.shape, F32)], name="middle",
    )


def middle_back_kernel(at_ref, parts_ref, h_ref, g_ref, gain_ref, low_ref, dh_ref, dg_ref):
    dg = jnp.zeros(dg_ref.shape, F32)
    for g in range(h_ref.shape[0]):
        e = sum_four(parts_ref, g)
        h = h_ref[g]
        r = lax.rsqrt(jnp.mean(h * h, axis=-1, keepdims=True) + EPS)
        unit = h * r
        ge = gain_ref[...] * e
        dh = g_ref[g].astype(F32) + r * (ge - unit * jnp.mean(ge * unit, axis=-1, keepdims=True))
        dh_ref[g] = dh
        write_four(low_ref, g, dh.astype(BF))
        dg += jnp.sum(e * unit, axis=0, keepdims=True)
    dg_ref[...] = dg


def middle_back(line, parts, h, grad, gain):
    return line.small(
        middle_back_kernel, parts, h, grad[0], gain,
        out_shape=[shape_of(parts.shape), shape_of(h.shape, F32), shape_of(gain.shape, F32)],
        name="middle_back",
    )


def finish_mixed_kernel(at_ref, parts_ref, h_ref, out_ref):
    for g in range(h_ref.shape[0]):
        out_ref[g] = (h_ref[g] + sum_four(parts_ref, g)).astype(BF)


def finish_mixed(line, parts, h):
    return line.small(
        finish_mixed_kernel, parts, h, out_shape=shape_of(h.shape), name="finish_mixed"
    )


def finish_tokens_kernel(at_ref, parts_ref, tok_ref, dh_ref, gain_ref, out_ref):
    for g in range(tok_ref.shape[0]):
        e = sum_four(parts_ref, g)
        v = tok_ref[g].astype(F32)
        r = lax.rsqrt(jnp.mean(v * v, axis=-1, keepdims=True) + EPS)
        unit = v * r
        ge = gain_ref[...] * e
        out_ref[g] = dh_ref[g] + r * (ge - unit * jnp.mean(ge * unit, axis=-1, keepdims=True))


def finish_tokens(line, parts, tok, dh, gain):
    return line.small(
        finish_tokens_kernel, parts, tok, dh, gain, out_shape=shape_of(dh.shape, F32), name="finish_tokens"
    )


def turn_kernel(at_ref, a_ref, b_ref, out_ref):
    rows = a_ref.shape[0]
    out_ref[:, :rows] = a_ref[...].astype(F32).T.astype(BF)
    out_ref[:, rows:] = b_ref[...].astype(F32).T.astype(BF)


def turn(line, pair):
    r, m = pair[0].shape
    block = 512
    columns = pl.BlockSpec((r, block), lambda k, at: (0, k))
    return line.call(
        turn_kernel, *pair,
        grid=(m // block,),
        in_specs=[columns, columns],
        out_specs=pl.BlockSpec((block, 2 * r), lambda k, at: (k, 0)),
        out_shape=shape_of((m, 2 * r)),
        name="turn",
    )


def both_rows(left_ref, ra_ref, rb_ref, at=slice(None)):
    rows = ra_ref.shape[0]
    return mm(left_ref[:, :rows], ra_ref[:, at]) + mm(left_ref[:, rows:], rb_ref[:, at])


def grad_kernel(start, begins, at_ref, left_ref, ra_ref, rb_ref, *refs):
    out_ref, acc_ref = refs[-2:]
    width = out_ref.shape[1]
    acc_ref[...] = both_rows(left_ref, ra_ref, rb_ref, slice(start, start + width))
    for begin, ref in zip(begins, refs):
        low, high = max(begin, start), min(begin + ref.shape[1], start + width)
        acc_ref[:, low - start : high - start] += ref[:, low - begin : high - begin].astype(F32)
    out_ref[...] = acc_ref[...].astype(BF)


def grad_whole_kernel(starts, final, at_ref, left_ref, ra_ref, rb_ref, *refs):
    out_ref, acc_ref = refs[-2:]

    def own():
        acc_ref[...] = both_rows(left_ref, ra_ref, rb_ref)
        for start, ref in zip(starts, refs):
            acc_ref[:, start : start + ref.shape[1]] += ref[...].astype(F32)
        out_ref[...] = acc_ref[...].astype(out_ref.dtype)

    if final:
        pl.when(pl.program_id(0) == 0)(own)

        @pl.when(pl.program_id(0) == 1)
        def _():
            out_ref[...] = refs[-3][...].astype(F32)
    else:
        own()


class WeightGrad:
    def __init__(self, line, left, right):
        self.line, self.left, self.right = line, left, right
        self.count = count = lax.axis_size("narrow")
        m, rows = left.shape
        self.r = rows // 2
        self.c = right[0][0].shape[1]
        self.block = m // count
        far = [bit for k in range(1, count.bit_length()) if (bit := count >> k) > TP_BIT]
        self.orders = {True: [1] + far, False: far + [1]}
        self.received = []

    def call(self, kernel, masks, extra, **kwargs):
        step = masks[1] - masks[0] if len(masks) > 1 else 0
        assert masks == [masks[0] + k * step for k in range(len(masks))]
        fixed = len(masks) == 1

        def which(k):
            return 0 if fixed else k

        arrays = [self.left, self.right[0][0], self.right[1][0]]
        specs = [
            pl.BlockSpec(
                (self.block, 2 * self.r), lambda k, at: (at[0] ^ (masks[0] + which(k) * step), 0)
            )
        ] + [pl.BlockSpec((self.r, self.c), lambda k, at, rows=rows: (rows, 0)) for _, rows in self.right]
        for array, begin, stride in extra:
            arrays.append(array)
            specs.append(
                pl.BlockSpec(
                    (None, self.block, array.shape[2]),
                    lambda k, at, begin=begin, stride=stride: (begin + which(k) * stride, 0, 0),
                )
            )
        return self.line.call(kernel, *arrays, in_specs=specs, name="grad", **kwargs)

    def send(self, stage, start=0, width=None, near_first=True):
        width = width or self.c
        order = self.orders[near_first]
        bit = order[stage]
        away = [k for k in range(self.count) if k & bit and not any(k & b for b in order[:stage])]
        extra, begins = [], []
        for masks, begin, size, array in self.received:
            if away[0] in masks and begin < start + width and start < begin + size:
                stride = masks.index(away[1]) - masks.index(away[0]) if len(away) > 1 else 0
                extra.append((array, masks.index(away[0]), stride))
                begins.append(begin)
        part = self.call(
            functools.partial(grad_kernel, start, begins), away, extra,
            grid=(len(away),),
            out_specs=pl.BlockSpec((None, self.block, width), lambda k, at: (k, 0, 0)),
            out_shape=shape_of((len(away), self.block, width)),
            scratch=[pltpu.VMEM((self.block, width), F32)],
        )
        got = swap(part, bit, 0)
        self.received.append(([k ^ bit for k in away], start, width, got))
        return got

    def rest(self, start=0, width=None):
        for stage in range(1, len(self.orders[True])):
            got = self.send(stage, start, width)
        return got

    def far(self, start=0, width=None):
        for stage in range(len(self.orders[False]) - 1):
            got = self.send(stage, start, width, False)
        return got

    def near(self, start=0, width=None):
        return self.send(len(self.orders[False]) - 1, start, width, False)

    def whole(self, mask, final, **kwargs):
        extra = [
            (array, masks.index(mask), 0)
            for masks, _, _, array in self.received
            if mask in masks
        ]
        starts = [begin for masks, begin, _, _ in self.received if mask in masks]
        if final:
            extra.append((self.peer, 0, 0))
        return self.call(
            functools.partial(grad_whole_kernel, starts, final), [mask], extra,
            scratch=[pltpu.VMEM((self.block, self.c), F32)], **kwargs,
        )

    def last(self):
        part = self.whole(
            TP_BIT, False,
            grid=(1,),
            out_specs=pl.BlockSpec((None, self.block, self.c), lambda k, at: (0, 0, 0)),
            out_shape=shape_of((1, self.block, self.c)),
        )
        self.peer = swap(part, TP_BIT, 0)

    def finish(self):
        return self.whole(
            0, True,
            grid=(2,),
            out_specs=pl.BlockSpec((self.block, self.c), lambda k, at: (0, k ^ at[2])),
            out_shape=shape_of((self.block, 2 * self.c), F32),
        )


def prepare_kernel(at_ref, q_ref, k_ref, v_ref, out_ref):
    width = k_ref.shape[1] // 2

    def own(ref):
        x = ref[...].astype(F32)
        return jnp.where(at_ref[2] == 0, x[:, :width], x[:, width:])

    x = jnp.concatenate([q_ref[...].astype(F32), own(k_ref), own(v_ref)], axis=1)
    out_ref[...] = x.T.astype(BF)


def prepare(line, w_query, w_key, w_value):
    m = w_query.shape[0]
    width, kv_width = w_query.shape[1] // 2, w_key.shape[1]
    rows = 512
    kv = pl.BlockSpec((rows, kv_width), lambda j, at: (j, 0))
    return line.call(
        prepare_kernel, w_query, w_key, w_value,
        grid=(m // rows,),
        in_specs=[pl.BlockSpec((rows, width), lambda j, at: (j, at[2])), kv, kv],
        out_specs=pl.BlockSpec((width + kv_width, rows), lambda j, at: (0, j)),
        out_shape=shape_of((width + kv_width, m)),
        name="prepare",
    )


def swap(x, narrow_mask, wide_mask):
    wide = lax.axis_size("wide")
    count = lax.axis_size("narrow") * wide
    mask = narrow_mask * wide + wide_mask
    return lax.ppermute(x, AXES, [(d, d ^ mask) for d in range(count)])


def chip_groups():
    wide = lax.axis_size("wide")
    count = lax.axis_size("narrow") * wide
    masks = (0, 2, TP_BIT * wide, TP_BIT * wide + 2)
    groups = sorted({tuple(sorted(d ^ mask for mask in masks)) for d in range(count)})
    return [list(group) for group in groups]


def exchange(x):
    return lax.all_to_all(x, AXES, 0, 0, tiled=True, axis_index_groups=chip_groups())


def gathered(x):
    a = exchange(x)
    return a, swap(a, 0, 1)


def scatter(line, a, b, shape):
    return exchange(chip_sum(line, a, b).reshape(shape))


def row_masks(count):
    return [(k & 1) | ((k >> 1) << 2) for k in range(count // 2)]


class Total:
    def __init__(self, x):
        self.x = x
        narrow = [1 << k for k in range(lax.axis_size("narrow").bit_length() - 1)]
        wide = [1 << k for k in range(lax.axis_size("wide").bit_length() - 1)]
        self.steps = [(0, k) for k in wide] + [(TP_BIT, 0)] + [(k, 0) for k in narrow if k != TP_BIT]

    def step(self, line):
        sent = swap(after(self.x, line.last[0]), *self.steps.pop(0))
        self.x = self.x + sent
        return sent

    def rest(self, line):
        while self.steps:
            self.step(line)
        return self.x


def after(x, *others):
    return lax.optimization_barrier((x, *others))[0]


def unit_rows(v):
    r = lax.rsqrt(jnp.mean(v * v, axis=-1, keepdims=True) + EPS)
    return v * r, r


def shards(
    tokens, lengths, attn_gain, w_query, key_matrix, value_matrix, q_gain, k_gain, w_out, ffn_gain,
    w_gate, w_up, w_down, out_grad,
):
    n, w = lax.axis_index("narrow"), lax.axis_index("wide")
    count = lax.axis_size("narrow")
    share, seqs, m = tokens.shape
    b = share * lax.axis_size("wide")
    half = (n // TP_BIT) % 2

    inside = position_inside(jnp.arange(b, dtype=jnp.int32), share, w)
    positions = jnp.stack([block_of(n, 0, i) * b + inside for i in range(2)]).astype(F32)
    freqs = jnp.exp(-math.log(10000.0) * jnp.arange(HALF, dtype=F32) * 2.0 / HEAD)
    angles = positions[:, None, :] * freqs[None, :, None]
    cos, sin = jnp.cos(angles), jnp.sin(angles)
    qg, kg = q_gain[:, None], k_gain[:, None]
    line = Line(jnp.concatenate([jnp.stack([n, w, half]).astype(jnp.int32), lengths]))
    masks = row_masks(count)
    rows = seqs * b
    shape = (4, seqs, share, m)

    def flat(pair):
        return tuple(x.reshape(rows, x.shape[-1]) for x in pair)

    def whole(pair):
        return tuple((x, 0) for x in flat(pair))

    def halves(x):
        return ((x, 0), (x, 1))

    tok = jnp.moveaxis(tokens, 1, 0)
    out_grad = jnp.moveaxis(out_grad, 1, 0)

    unit, _ = unit_rows(tok.astype(F32))
    sent = exchange(jnp.broadcast_to((unit * attn_gain).astype(BF)[None], shape))
    grad = mask(line, out_grad, b)
    wt = prepare(line, w_query, key_matrix, value_matrix)
    sent = after(sent, wt)
    xn = (sent, swap(sent, 0, 1))
    g_own = exchange(after(grad, sent))
    kv, q, raw = project(line, xn, wt, cos, sin, qg, kg)
    kvs = [swap(kv, k, 0) if k else kv for k in masks]
    xn_turned = turn(line, flat(xn))
    line.wait(g_own)
    pb, pa, oa, ob, log = attend(line, q, kvs, masks, w_out, share)
    pb = swap(pb, 0, 1)
    g_all = (g_own, swap(g_own, 0, 1))
    parts = scatter(line, *flat((pa, pb)), shape)
    g_turned = turn(line, flat(g_all))
    hn, h = middle(line, parts, tok, ffn_gain[None])
    hn = gathered(hn)

    db, da, act, dgate, dup = ffn(line, flat(hn), flat(g_all), w_gate, w_up, w_down)
    db = swap(db, 0, 1)
    c = act.shape[1]
    first, rest = (0, c // 4), (c // 4, 3 * c // 4)
    early, late = (0, 3 * c // 8), (3 * c // 8, 5 * c // 8)
    d_down = WeightGrad(line, g_turned, halves(act))
    d_down.send(0)
    parts = scatter(line, da, db, shape)
    hn_turned = turn(line, flat(hn))
    d_gate = WeightGrad(line, hn_turned, halves(dgate))
    d_up = WeightGrad(line, hn_turned, halves(dup))
    u_first = d_up.far(*early)
    g_first = d_gate.send(0, *first)
    g_rest = d_gate.send(0, *rest)
    dhl, dh, ffn_gain_grad = middle_back(line, parts, h, grad, ffn_gain[None])
    dhl = exchange(dhl)
    line.wait(u_first)
    d_first = d_down.rest(*first)
    yb, ya = down(line, act, w_down)
    yb = swap(yb, 0, 1)
    d_rest = d_down.rest(*rest)
    dhl = after(dhl, line.last[0], g_first, d_first, yb)
    dhl = (dhl, swap(dhl, 0, 1))
    mixed_parts = scatter(line, ya, yb, shape)

    back = attend_back(line, dhl, q, kvs, masks, w_out, (oa, ob), log, raw, cos, sin, qg, share)
    dq, dkvs, dqg = back[:2], after(tuple(back[2:-1]), g_rest, d_rest), back[-1]
    dkvs = [swap(x, k, 0) if k else x for x, k in zip(dkvs, masks)]
    dhl_turned = turn(line, flat(dhl))
    dxb, dxa, dwa, dwb, dkg, dag = project_back(line, dkvs, dq, raw, xn, wt, cos, sin, kg)
    dxb = swap(dxb, 0, 1)
    mixed = finish_mixed(line, mixed_parts, h)
    parts = scatter(line, *flat((dxa, dxb)), shape)
    g_z = d_gate.rest()
    d_up.send(0, *late)
    d_qkv = WeightGrad(line, xn_turned, whole((dwa, dwb)))
    d_qkv.send(0)
    d_out = WeightGrad(line, dhl_turned, whole((oa, ob)))
    d_out.send(0)
    d_up.near(*early)
    gains = jnp.concatenate(
        [dag[0] / attn_gain, ffn_gain_grad[0], jnp.sum(dqg, axis=1), jnp.sum(dkg, axis=1)]
    )
    gains = Total(gains.reshape(-1, 128))
    sent = gains.step(line)
    d_down.last()
    line.wait(g_z, sent)
    d_tokens = finish_tokens(line, parts, tok, dh, attn_gain[None])
    sent = gains.step(line)
    d_qkv.rest()
    d_out.rest()
    u_z = d_up.rest(*late)
    d_gate.last()
    down_grad = d_down.finish()
    line.wait(sent)
    d_qkv.last()
    sent = gains.step(line)
    gate_grad = d_gate.finish()
    line.wait(u_z)
    d_up.last()
    d_out.last()
    line.wait(sent)
    qkv_grad = d_qkv.finish()
    sent = gains.step(line)
    out_grad_t = d_out.finish()
    line.wait(sent)
    up_grad = d_up.finish()
    gains = gains.rest(line).reshape(-1)
    width = dq[0].shape[3]
    columns = dwa.shape[3]
    qkv_grad = qkv_grad.reshape(-1, 2, columns)
    query_grad = qkv_grad[:, :, :width].reshape(-1, 2 * width)
    return (
        jnp.moveaxis(mixed, 0, 1),
        jnp.moveaxis(d_tokens, 0, 1),
        gains[:m],
        query_grad,
        qkv_grad[:, :, width : width + HEAD].reshape(-1, 2 * HEAD),
        qkv_grad[:, :, width + HEAD :].reshape(-1, 2 * HEAD),
        gains[2 * m : 2 * m + HEAD],
        gains[2 * m + HEAD :],
        out_grad_t,
        gains[m : 2 * m],
        gate_grad,
        up_grad,
        down_grad,
    )


def solution(mesh):
    rows = P(AXES, None, None)
    columns = P(None, "wide")
    block = P("narrow", "wide")
    in_specs = (
        rows, P(), P(), columns, columns, columns, P(), P(), P("wide", None), P(), columns, columns,
        P("wide", None), rows,
    )
    out_specs = (
        rows, rows, P(), block, block, block, P(), P(), block, P(), block, block, block,
    )
    return jax.shard_map(shards, mesh=mesh, in_specs=in_specs, out_specs=out_specs, check_vma=False)
```

```python
import functools
import math

import jax
import jax.numpy as jnp
from jax import lax
from jax.experimental import pallas as pl
from jax.experimental.pallas import tpu as pltpu
from jax.sharding import PartitionSpec as P

QUERY_HEADS = 32
KEY_VALUE_HEADS = 8
HEAD = 64
HALF = HEAD // 2
GROUP = QUERY_HEADS // KEY_VALUE_HEADS
EPS = 1e-06
SCALE = HEAD ** (-0.5)
AXES = ("narrow", "wide")
TP_BIT = 2
BF = jnp.bfloat16
F32 = jnp.float32
MIB = 2**20
KERNEL_FLOPS = 3 * 10**9

NN = (((1,), (0,)), ((), ()))
NT = (((1,), (1,)), ((), ()))
TN = (((0,), (0,)), ((), ()))


def mm(a, b, dims=NN):
    return lax.dot_general(a, b, dims, preferred_element_type=F32)


class Line:
    def __init__(self, at):
        self.at = at
        self.last = []
        self.needed = []

    def wait(self, *arrays):
        self.needed += arrays

    def call(self, kernel, *args, grid, in_specs, out_specs, out_shape, scratch=(), name=None, limit=52 * 2**20):
        extra = [*self.last, *self.needed]
        self.needed = []

        def body(at_ref, *refs):
            kernel(at_ref, *refs[len(extra) :])

        outs = pl.pallas_call(
            body,
            grid_spec=pltpu.PrefetchScalarGridSpec(
                num_scalar_prefetch=1,
                grid=grid,
                in_specs=[pl.BlockSpec(memory_space=pl.ANY)] * len(extra) + list(in_specs),
                out_specs=out_specs,
                scratch_shapes=scratch,
            ),
            out_shape=out_shape,
            compiler_params=pltpu.CompilerParams(vmem_limit_bytes=limit),
            cost_estimate=pl.CostEstimate(flops=KERNEL_FLOPS, bytes_accessed=0, transcendentals=0),
            name=name,
        )(self.at, *extra, *args)
        self.last = [outs[0] if isinstance(outs, (list, tuple)) else outs]
        return outs

    def small(self, kernel, *args, out_shape, name):
        spec = pl.BlockSpec(memory_space=pltpu.VMEM)
        outs = jax.tree.map(lambda _: spec, out_shape)
        return self.call(
            kernel, *args,
            grid=(), in_specs=[spec] * len(args), out_specs=outs, out_shape=out_shape, limit=8 * MIB, name=name,
        )


def position_inside(t, share, w):
    u = t // share
    return (((u & 1) << 1) | ((u >> 1) ^ (w & 1))) * share + t % share


def block_of(n, mask, i):
    return ((n ^ mask) & ~TP_BIT) | (TP_BIT * i)


def join(ref):
    return jnp.concatenate([ref[0, 0], ref[1, 0]], axis=0)


def split(ref, value):
    share = ref.shape[2]
    ref[0, 0] = value[:share]
    ref[1, 0] = value[share:]


def positions_in_block(size, share, w, axis):
    shape = (size, 1) if axis == 0 else (1, size)
    return position_inside(lax.broadcasted_iota(jnp.int32, shape, axis), share, w)


def constant(shape):
    return pl.BlockSpec(shape, lambda *_: (0,) * len(shape))


def per_block(shape):
    return pl.BlockSpec(shape, lambda g, i, at: (g, i) + (0,) * (len(shape) - 2))


def chips(share, columns):
    return pl.BlockSpec((2, 1, share, columns), lambda g, i, at: (i, g, 0, 0))


def per_sequence(shape):
    return pl.BlockSpec(shape, lambda g, *_: (g,) + (0,) * (len(shape) - 1))


def shape_of(shape, dtype=BF):
    return jax.ShapeDtypeStruct(shape, dtype)


def project_kernel(at_ref, a_ref, b_ref, wt_ref, cos_ref, sin_ref, qg_ref, kg_ref, kv_ref, q_ref, raw_ref):
    x = jnp.concatenate([join(a_ref), join(b_ref)], axis=0)
    y = mm(wt_ref[...], x, NT)
    heads = y.shape[0] // HEAD - 2
    width = heads * HEAD
    raw_ref[0, 0] = y[: width + HEAD]
    c, s = cos_ref[0], sin_ref[0]

    def norm_rope(v, gain):
        r = lax.rsqrt(jnp.mean(v * v, axis=0, keepdims=True) + EPS)
        n = v * r * gain
        a, b = n[:HALF], n[HALF:]
        return a * c - b * s, b * c + a * s

    q = []
    for h in range(heads):
        a, b = norm_rope(y[h * HEAD : (h + 1) * HEAD], qg_ref[...])
        q.append(jnp.concatenate([a, b], axis=0) * SCALE)
    q_ref[0, 0] = jnp.concatenate(q, axis=1).astype(BF)
    a, b = norm_rope(y[width : width + HEAD], kg_ref[...])
    kv = jnp.concatenate([a, b, y[width + HEAD :]], axis=0)
    kv_ref[0] = kv.T.astype(BF)


def project(line, xn, wt, cos, sin, q_gain, k_gain):
    _, g, share, m = xn[0].shape
    b = 4 * share
    c = wt.shape[0]
    heads = c // HEAD - 2
    table = pl.BlockSpec((1, HALF, b), lambda g, i, at: (i, 0, 0))
    return line.call(
        project_kernel, *xn, wt, cos, sin, q_gain, k_gain,
        grid=(g, 2),
        in_specs=[chips(share, m)] * 2
        + [constant((c, m)), table, table, constant((HEAD, 1)), constant((HEAD, 1))],
        out_specs=[
            per_block((1, b, 2 * HEAD)),
            per_block((1, 1, HEAD, heads * b)),
            per_block((1, 1, (heads + 1) * HEAD, b)),
        ],
        out_shape=[
            shape_of((g, 2 * b, 2 * HEAD)),
            shape_of((g, 2, HEAD, heads * b)),
            shape_of((g, 2, (heads + 1) * HEAD, b), F32),
        ],
        name="project",
    )


def attend_kernel(masks, share, at_ref, q_ref, *refs):
    kv_refs = refs[: len(masks)]
    wo_ref, pb_ref, pa_ref, oa_ref, ob_ref, log_ref, acc_ref = refs[len(masks) :]
    n, w = at_ref[0], at_ref[1]
    length = at_ref[3 + pl.program_id(0)]
    b = kv_refs[0].shape[1] // 2
    heads = q_ref.shape[3] // b
    nq = block_of(n, 0, pl.program_id(1))
    bound = jnp.minimum(nq * b + positions_in_block(b, share, w, 1), length - 1)
    bound = jnp.concatenate([bound] * heads, axis=1)
    acc_ref[...] = jnp.zeros_like(acc_ref)
    inside = positions_in_block(b, share, w, 0)
    low = lax.broadcasted_iota(jnp.int32, (b, 2 * HEAD), 1) < HEAD

    for k, kv_ref in enumerate(kv_refs):
        for tp in range(2):
            nk = block_of(n, masks[k], tp)

            def add(masked):
                kv = kv_ref[0, tp * b : (tp + 1) * b, :]
                p = jnp.exp(mm(kv[:, :HEAD], q_ref[0, 0]))
                if masked:
                    p = jnp.where(nk * b + inside <= bound, p, 0.0)
                acc_ref[...] += mm(jnp.where(low, jnp.ones_like(kv), kv), p.astype(BF), TN)

            whole = (nk < nq) & ((nk + 1) * b <= length)
            pl.when(whole)(functools.partial(add, False))
            pl.when((nk <= nq) & (nk * b < length) & jnp.logical_not(whole))(functools.partial(add, True))

    total = acc_ref[:1, :]
    log_ref[0, 0] = jnp.log(total)
    o = acc_ref[HEAD:, :] / total
    o = jnp.concatenate([o[:, h * b : (h + 1) * b] for h in range(heads)], axis=0).T.astype(BF)
    split(oa_ref, o[: b // 2])
    split(ob_ref, o[b // 2 :])
    part = mm(o, wo_ref[...]).astype(BF)
    split(pa_ref, part[: b // 2])
    split(pb_ref, part[b // 2 :])


def attend(line, q, kvs, masks, w_out, share):
    g, b = q.shape[0], kvs[0].shape[1] // 2
    heads = q.shape[3] // b
    m = w_out.shape[1]
    width = heads * HEAD
    return line.call(
        functools.partial(attend_kernel, masks, share), q, *kvs, w_out,
        grid=(g, 2),
        in_specs=[per_block((1, 1, HEAD, heads * b))]
        + [per_sequence((1, 2 * b, 2 * HEAD))] * len(kvs)
        + [pl.BlockSpec((width, m), lambda g, i, at: (at[2], 0))],
        out_specs=[chips(share, m)] * 2
        + [chips(share, width)] * 2
        + [per_block((1, 1, 1, heads * b))],
        out_shape=[shape_of((4, g, share, m))] * 2
        + [shape_of((4, g, share, width))] * 2
        + [shape_of((g, 2, 1, heads * b), F32)],
        scratch=[pltpu.VMEM((2 * HEAD, heads * b), F32)],
        name="attend",
    )


def attend_back_kernel(masks, share, at_ref, dha_ref, dhb_ref, q_ref, *refs):
    count = len(masks)
    kv_refs, refs = refs[:count], refs[count:]
    wo_ref, oa_ref, ob_ref, log_ref, raw_ref, cos_ref, sin_ref, qg_ref, dqa_ref, dqb_ref = refs[:10]
    dkv_refs, dqg_ref = refs[10 : 10 + count], refs[10 + count]
    q_ext, do_ext, delta, dq_acc, dkv_acc = refs[11 + count :]
    n, w = at_ref[0], at_ref[1]
    at_g, i = pl.program_id(0), pl.program_id(1)
    length = at_ref[3 + at_g]
    b = kv_refs[0].shape[1] // 2
    heads = q_ref.shape[3] // b
    nq = block_of(n, 0, i)
    bound = jnp.minimum(nq * b + positions_in_block(b, share, w, 1), length - 1)
    bound = jnp.concatenate([bound] * heads, axis=1)
    inside = positions_in_block(b, share, w, 0)

    @pl.when(i == 0)
    def _():
        dkv_acc[...] = jnp.zeros_like(dkv_acc)

    @pl.when((i == 0) & (at_g == 0))
    def _():
        dqg_ref[...] = jnp.zeros_like(dqg_ref)

    dq_acc[...] = jnp.zeros_like(dq_acc)

    @pl.when(nq * b < length)
    def _():
        dh = jnp.concatenate([join(dha_ref), join(dhb_ref)], axis=0)
        do = mm(wo_ref[...], dh, NT).astype(BF).astype(F32)
        o = jnp.concatenate([join(oa_ref), join(ob_ref)], axis=0).astype(F32).T

        def heads_side_by_side(x):
            return jnp.concatenate([x[h * HEAD : (h + 1) * HEAD] for h in range(heads)], axis=1)

        do = heads_side_by_side(do)
        delta[...] = jnp.sum(do * heads_side_by_side(o), axis=0, keepdims=True)
        none = jnp.zeros((HEAD, heads * b), BF)
        do_ext[...] = jnp.concatenate([none, do.astype(BF)], axis=0)
        q_ext[...] = jnp.concatenate([q_ref[0, 0], none], axis=0)

    for k, kv_ref in enumerate(kv_refs):
        for tp in range(2):
            nk = block_of(n, masks[k], tp)

            def add(masked):
                kv = kv_ref[0, tp * b : (tp + 1) * b, :]
                p = jnp.exp(mm(kv, q_ext[...]) - log_ref[0, 0])
                if masked:
                    p = jnp.where(nk * b + inside <= bound, p, 0.0)
                ds = (p * (mm(kv, do_ext[...]) - delta[...])).astype(BF)
                dq_acc[...] += mm(kv, ds, TN)
                rows = slice((2 * k + tp) * b, (2 * k + tp + 1) * b)
                dkv_acc[rows, :] += mm(ds, q_ext[...], NT) + mm(p.astype(BF), do_ext[...], NT)

            whole = (nk < nq) & ((nk + 1) * b <= length)
            seen = (nk <= nq) & (nk * b < length) & (nq * b < length)
            pl.when(seen & whole)(functools.partial(add, False))
            pl.when(seen & jnp.logical_not(whole))(functools.partial(add, True))

    c, s = cos_ref[0], sin_ref[0]
    parts = []
    gain_sum = jnp.zeros((HEAD, b), F32)
    for h in range(heads):
        dq = dq_acc[:HEAD, h * b : (h + 1) * b] * SCALE
        e1, e2 = dq[:HALF], dq[HALF:]
        e = jnp.concatenate([e1 * c + e2 * s, e2 * c - e1 * s], axis=0)
        v = raw_ref[0, 0, h * HEAD : (h + 1) * HEAD, :]
        r = lax.rsqrt(jnp.mean(v * v, axis=0, keepdims=True) + EPS)
        unit = v * r
        ge = qg_ref[...] * e
        parts.append(r * (ge - unit * jnp.mean(ge * unit, axis=0, keepdims=True)))
        gain_sum += e * unit
    dq = jnp.concatenate(parts, axis=0).T.astype(BF)
    split(dqa_ref, dq[: b // 2])
    split(dqb_ref, dq[b // 2 :])
    dqg_ref[...] += gain_sum

    @pl.when(i == 1)
    def _():
        for k, ref in enumerate(dkv_refs):
            ref[0] = dkv_acc[2 * k * b : 2 * (k + 1) * b, :].astype(BF)


def attend_back(line, dh, q, kvs, masks, w_out, o, log, raw, cos, sin, q_gain, share):
    g, b = q.shape[0], kvs[0].shape[1] // 2
    heads = q.shape[3] // b
    m = w_out.shape[1]
    width = heads * HEAD
    half_rows = chips(share, width)
    table = pl.BlockSpec((1, HALF, b), lambda g, i, at: (i, 0, 0))
    return line.call(
        functools.partial(attend_back_kernel, masks, share),
        *dh, q, *kvs, w_out, *o, log, raw, cos, sin, q_gain,
        grid=(g, 2),
        in_specs=[chips(share, m)] * 2
        + [per_block((1, 1, HEAD, heads * b))]
        + [per_sequence((1, 2 * b, 2 * HEAD))] * len(kvs)
        + [
            pl.BlockSpec((width, m), lambda g, i, at: (at[2], 0)),
            half_rows,
            half_rows,
            per_block((1, 1, 1, heads * b)),
            per_block((1, 1, width, b)),
            table,
            table,
            constant((HEAD, 1)),
        ],
        out_specs=[half_rows, half_rows]
        + [per_sequence((1, 2 * b, 2 * HEAD))] * len(kvs)
        + [constant((HEAD, b))],
        scratch=[
            pltpu.VMEM((2 * HEAD, heads * b), BF),
            pltpu.VMEM((2 * HEAD, heads * b), BF),
            pltpu.VMEM((1, heads * b), F32),
            pltpu.VMEM((2 * HEAD, heads * b), F32),
            pltpu.VMEM((2 * b * len(kvs), 2 * HEAD), F32),
        ],
        out_shape=[shape_of((4, g, share, width))] * 2
        + [shape_of((g, 2 * b, 2 * HEAD))] * len(kvs)
        + [shape_of((HEAD, b), F32)],
        name="attend_back",
    )


def project_back_kernel(count, at_ref, *refs):
    dkv_refs = refs[:count]
    (
        dqa_ref, dqb_ref, raw_ref, xa_ref, xb_ref, wt_ref, cos_ref, sin_ref, kg_ref,
        dxb_ref, dxa_ref, dwa_ref, dwb_ref, dkg_ref, dag_ref,
    ) = refs[count:]

    @pl.when((pl.program_id(0) == 0) & (pl.program_id(1) == 0))
    def _():
        dkg_ref[...] = jnp.zeros_like(dkg_ref)
        dag_ref[...] = jnp.zeros_like(dag_ref)

    total = dkv_refs[0][0].astype(F32)
    for ref in dkv_refs[1:]:
        total += ref[0].astype(F32)
    t = total.T
    half = total.shape[0] // 2
    c, s = cos_ref[0], sin_ref[0]
    e1, e2 = t[:HALF], t[HALF:HEAD]
    e = jnp.concatenate([e1 * c + e2 * s, e2 * c - e1 * s], axis=0)
    v = raw_ref[0, 0]
    r = lax.rsqrt(jnp.mean(v * v, axis=0, keepdims=True) + EPS)
    unit = v * r
    ge = kg_ref[...] * e
    dk = r * (ge - unit * jnp.mean(ge * unit, axis=0, keepdims=True))
    dkg_ref[...] += e * unit
    dkv = jnp.concatenate([dk, t[HEAD:]], axis=0).T.astype(BF)
    width = dqa_ref.shape[3]
    gain_sum = jnp.zeros(dag_ref.shape, F32)
    for rows, dq_ref, x_ref, dx_ref, dw_ref in (
        (slice(0, half), dqa_ref, xa_ref, dxa_ref, dwa_ref),
        (slice(half, 2 * half), dqb_ref, xb_ref, dxb_ref, dwb_ref),
    ):
        dqkv = jnp.concatenate([join(dq_ref), dkv[rows]], axis=1)
        split(dw_ref, dqkv)
        dx = mm(dqkv, wt_ref[...])
        split(dx_ref, dx.astype(BF))
        gain_sum += jnp.sum(dx * join(x_ref).astype(F32), axis=0, keepdims=True)
    dag_ref[...] += gain_sum


def project_back(line, dkvs, dq, raw, xn, wt, cos, sin, k_gain):
    _, g, share, m = xn[0].shape
    b = 4 * share
    c = wt.shape[0]
    width = dq[0].shape[3]
    heads = width // HEAD
    table = pl.BlockSpec((1, HALF, b), lambda g, i, at: (i, 0, 0))
    return line.call(
        functools.partial(project_back_kernel, len(dkvs)),
        *dkvs, *dq, raw, *xn, wt, cos, sin, k_gain,
        grid=(g, 2),
        in_specs=[per_block((1, b, 2 * HEAD))] * len(dkvs)
        + [chips(share, width)] * 2
        + [pl.BlockSpec((1, 1, HEAD, b), lambda g, i, at: (g, i, heads, 0))]
        + [chips(share, m)] * 2
        + [constant((c, m)), table, table, constant((HEAD, 1))],
        out_specs=[chips(share, m)] * 2
        + [chips(share, c)] * 2
        + [constant((HEAD, b)), constant((1, m))],
        out_shape=[shape_of((4, g, share, m))] * 2
        + [shape_of((4, g, share, c))] * 2
        + [shape_of((HEAD, b), F32), shape_of((1, m), F32)],
        name="project_back",
    )


def ffn_kernel(
    tiles, at_ref, ha_ref, hb_ref, ga_ref, gb_ref, wg_ref, wu_ref, wd_ref, wgr_ref, wur_ref,
    db_ref, da_ref, act_ref, dgate_ref, dup_ref, keep_ref,
):
    t = pl.program_id(0)
    rows = ha_ref.shape[0]

    @pl.when(t < tiles)
    def _():
        for k, (h_ref, g_ref) in enumerate(((ha_ref, ga_ref), (hb_ref, gb_ref))):
            at = slice(k * rows, (k + 1) * rows)
            gate = mm(h_ref[...], wg_ref[...])
            up = mm(h_ref[...], wu_ref[...])
            dact = mm(g_ref[...], wd_ref[...], NT)
            sig = 1.0 / (1.0 + jnp.exp(-gate))
            silu = gate * sig
            act_ref[at, :] = (silu * up).astype(BF)
            dgate = (dact * up * (sig * (1.0 + gate * (1.0 - sig)))).astype(BF)
            dup = (dact * silu).astype(BF)
            dgate_ref[at, :] = dgate
            dup_ref[at, :] = dup
            keep_ref[t, 0, at, :] = dgate
            keep_ref[t, 1, at, :] = dup

    @pl.when(t >= tiles)
    def _():
        tile = keep_ref.shape[3]
        for k, d_ref in enumerate((da_ref, db_ref)):
            at = slice(k * rows, (k + 1) * rows)
            total = None
            for u in range(tiles):
                columns = slice(u * tile, (u + 1) * tile)
                part = mm(keep_ref[u, 0, at, :], wgr_ref[:, columns], NT)
                part += mm(keep_ref[u, 1, at, :], wur_ref[:, columns], NT)
                total = part if total is None else total + part
            d_ref[...] = total.astype(BF)


def ffn(line, hn, g, w_gate, w_up, w_down):
    r, m = hn[0].shape
    hidden = w_gate.shape[1] // 2
    tile, block = 256, 256
    tiles = hidden // tile

    def forward(t):
        return jnp.minimum(t, tiles - 1)

    def backward(t):
        return jnp.maximum(t - tiles, 0)

    columns = pl.BlockSpec((m, tile), lambda t, at: (0, at[2] * tiles + forward(t)))
    block_rows = pl.BlockSpec((block, hidden), lambda t, at: (backward(t), at[2]))
    d_block = pl.BlockSpec((r, block), lambda t, at: (0, backward(t)))
    hidden_block = pl.BlockSpec((2 * r, tile), lambda t, at: (0, forward(t)))
    return line.call(
        functools.partial(ffn_kernel, tiles), *hn, *g, w_gate, w_up, w_down, w_gate, w_up,
        grid=(tiles + m // block,),
        in_specs=[constant((r, m))] * 4
        + [
            columns,
            columns,
            pl.BlockSpec((tile, m), lambda t, at: (at[2] * tiles + forward(t), 0)),
            block_rows,
            block_rows,
        ],
        out_specs=[d_block, d_block, hidden_block, hidden_block, hidden_block],
        scratch=[pltpu.VMEM((tiles, 2, 2 * r, tile), BF)],
        out_shape=[shape_of((r, m))] * 2 + [shape_of((2 * r, hidden))] * 3,
        name="ffn",
        limit=52 * MIB,
    )


def down_kernel(at_ref, act_ref, wd_ref, b_ref, a_ref):
    r = a_ref.shape[0]
    y = mm(act_ref[...], wd_ref[...]).astype(BF)
    a_ref[...] = y[:r]
    b_ref[...] = y[r:]


def down(line, act, w_down):
    rows, hidden = act.shape
    m = w_down.shape[1]
    block = 256
    out = pl.BlockSpec((rows // 2, block), lambda t, at: (0, t))
    return line.call(
        down_kernel, act, w_down,
        grid=(m // block,),
        in_specs=[
            constant((rows, hidden)),
            pl.BlockSpec((hidden, block), lambda t, at: (at[2], t)),
        ],
        out_specs=[out, out],
        out_shape=[shape_of((rows // 2, m))] * 2,
        name="down",
    )


def chip_sum_kernel(at_ref, a_ref, b_ref, out_ref):
    rows = out_ref.shape[0]
    for k in range(0, rows, rows // 8):
        at = slice(k, k + rows // 8)
        out_ref[at] = (a_ref[at].astype(F32) + b_ref[at].astype(F32)).astype(BF)


def chip_sum(line, a, b):
    return line.small(chip_sum_kernel, a, b, out_shape=shape_of(a.shape), name="chip_sum")


def write_four(ref, g, value):
    for k in range(4):
        ref[k, g] = value


def sum_four(ref, g):
    total = ref[0, g].astype(F32)
    for k in range(1, 4):
        total += ref[k, g].astype(F32)
    return total


def mask_kernel(n_rows, at_ref, g_ref, out_ref):
    seqs, share, _ = g_ref.shape
    first = at_ref[0] * n_rows + at_ref[1] * share
    p = first + lax.broadcasted_iota(jnp.int32, (share, 1), 0)
    for g in range(seqs):
        write_four(out_ref, g, jnp.where(p < at_ref[3 + g], g_ref[g].astype(F32), 0.0).astype(BF))


def mask(line, grad, b):
    g, share, m = grad.shape
    return line.small(
        functools.partial(mask_kernel, b), grad, out_shape=shape_of((4, g, share, m)), name="mask"
    )


def middle_kernel(at_ref, parts_ref, tok_ref, gain_ref, hn_ref, h_ref):
    for g in range(tok_ref.shape[0]):
        h = tok_ref[g].astype(F32) + sum_four(parts_ref, g)
        h_ref[g] = h
        r = lax.rsqrt(jnp.mean(h * h, axis=-1, keepdims=True) + EPS)
        write_four(hn_ref, g, (h * r * gain_ref[...]).astype(BF))


def middle(line, parts, tok, gain):
    return line.small(
        middle_kernel, parts, tok, gain,
        out_shape=[shape_of(parts.shape), shape_of(tok.shape, F32)], name="middle",
    )


def middle_back_kernel(at_ref, parts_ref, h_ref, g_ref, gain_ref, low_ref, dh_ref, dg_ref):
    dg = jnp.zeros(dg_ref.shape, F32)
    for g in range(h_ref.shape[0]):
        e = sum_four(parts_ref, g)
        h = h_ref[g]
        r = lax.rsqrt(jnp.mean(h * h, axis=-1, keepdims=True) + EPS)
        unit = h * r
        ge = gain_ref[...] * e
        dh = g_ref[g].astype(F32) + r * (ge - unit * jnp.mean(ge * unit, axis=-1, keepdims=True))
        dh_ref[g] = dh
        write_four(low_ref, g, dh.astype(BF))
        dg += jnp.sum(e * unit, axis=0, keepdims=True)
    dg_ref[...] = dg


def middle_back(line, parts, h, grad, gain):
    return line.small(
        middle_back_kernel, parts, h, grad[0], gain,
        out_shape=[shape_of(parts.shape), shape_of(h.shape, F32), shape_of(gain.shape, F32)],
        name="middle_back",
    )


def finish_mixed_kernel(at_ref, parts_ref, h_ref, out_ref):
    for g in range(h_ref.shape[0]):
        out_ref[g] = (h_ref[g] + sum_four(parts_ref, g)).astype(BF)


def finish_mixed(line, parts, h):
    return line.small(
        finish_mixed_kernel, parts, h, out_shape=shape_of(h.shape), name="finish_mixed"
    )


def finish_tokens_kernel(at_ref, parts_ref, tok_ref, dh_ref, gain_ref, out_ref):
    for g in range(tok_ref.shape[0]):
        e = sum_four(parts_ref, g)
        v = tok_ref[g].astype(F32)
        r = lax.rsqrt(jnp.mean(v * v, axis=-1, keepdims=True) + EPS)
        unit = v * r
        ge = gain_ref[...] * e
        out_ref[g] = dh_ref[g] + r * (ge - unit * jnp.mean(ge * unit, axis=-1, keepdims=True))


def finish_tokens(line, parts, tok, dh, gain):
    return line.small(
        finish_tokens_kernel, parts, tok, dh, gain, out_shape=shape_of(dh.shape, F32), name="finish_tokens"
    )


def turn_kernel(at_ref, a_ref, b_ref, out_ref):
    rows = a_ref.shape[0]
    out_ref[:, :rows] = a_ref[...].astype(F32).T.astype(BF)
    out_ref[:, rows:] = b_ref[...].astype(F32).T.astype(BF)


def turn(line, pair):
    r, m = pair[0].shape
    block = 512
    columns = pl.BlockSpec((r, block), lambda k, at: (0, k))
    return line.call(
        turn_kernel, *pair,
        grid=(m // block,),
        in_specs=[columns, columns],
        out_specs=pl.BlockSpec((block, 2 * r), lambda k, at: (k, 0)),
        out_shape=shape_of((m, 2 * r)),
        name="turn",
    )


def both_rows(left_ref, ra_ref, rb_ref, at=slice(None)):
    rows = ra_ref.shape[0]
    return mm(left_ref[:, :rows], ra_ref[:, at]) + mm(left_ref[:, rows:], rb_ref[:, at])


def grad_kernel(start, begins, at_ref, left_ref, ra_ref, rb_ref, *refs):
    out_ref, acc_ref = refs[-2:]
    width = out_ref.shape[1]
    acc_ref[...] = both_rows(left_ref, ra_ref, rb_ref, slice(start, start + width))
    for begin, ref in zip(begins, refs):
        low, high = max(begin, start), min(begin + ref.shape[1], start + width)
        acc_ref[:, low - start : high - start] += ref[:, low - begin : high - begin].astype(F32)
    out_ref[...] = acc_ref[...].astype(BF)


def grad_whole_kernel(starts, final, at_ref, left_ref, ra_ref, rb_ref, *refs):
    out_ref, acc_ref = refs[-2:]

    def own():
        acc_ref[...] = both_rows(left_ref, ra_ref, rb_ref)
        for start, ref in zip(starts, refs):
            acc_ref[:, start : start + ref.shape[1]] += ref[...].astype(F32)
        out_ref[...] = acc_ref[...].astype(out_ref.dtype)

    if final:
        pl.when(pl.program_id(0) == 0)(own)

        @pl.when(pl.program_id(0) == 1)
        def _():
            out_ref[...] = refs[-3][...].astype(F32)
    else:
        own()


class WeightGrad:
    def __init__(self, line, left, right):
        self.line, self.left, self.right = line, left, right
        self.count = count = lax.axis_size("narrow")
        m, rows = left.shape
        self.r = rows // 2
        self.c = right[0][0].shape[1]
        self.block = m // count
        far = [bit for k in range(1, count.bit_length()) if (bit := count >> k) > TP_BIT]
        self.orders = {True: [1] + far, False: far + [1]}
        self.received = []

    def call(self, kernel, masks, extra, **kwargs):
        step = masks[1] - masks[0] if len(masks) > 1 else 0
        assert masks == [masks[0] + k * step for k in range(len(masks))]
        fixed = len(masks) == 1

        def which(k):
            return 0 if fixed else k

        arrays = [self.left, self.right[0][0], self.right[1][0]]
        specs = [
            pl.BlockSpec(
                (self.block, 2 * self.r), lambda k, at: (at[0] ^ (masks[0] + which(k) * step), 0)
            )
        ] + [pl.BlockSpec((self.r, self.c), lambda k, at, rows=rows: (rows, 0)) for _, rows in self.right]
        for array, begin, stride in extra:
            arrays.append(array)
            specs.append(
                pl.BlockSpec(
                    (None, self.block, array.shape[2]),
                    lambda k, at, begin=begin, stride=stride: (begin + which(k) * stride, 0, 0),
                )
            )
        return self.line.call(kernel, *arrays, in_specs=specs, name="grad", **kwargs)

    def send(self, stage, start=0, width=None, near_first=True):
        width = width or self.c
        order = self.orders[near_first]
        bit = order[stage]
        away = [k for k in range(self.count) if k & bit and not any(k & b for b in order[:stage])]
        extra, begins = [], []
        for masks, begin, size, array in self.received:
            if away[0] in masks and begin < start + width and start < begin + size:
                stride = masks.index(away[1]) - masks.index(away[0]) if len(away) > 1 else 0
                extra.append((array, masks.index(away[0]), stride))
                begins.append(begin)
        part = self.call(
            functools.partial(grad_kernel, start, begins), away, extra,
            grid=(len(away),),
            out_specs=pl.BlockSpec((None, self.block, width), lambda k, at: (k, 0, 0)),
            out_shape=shape_of((len(away), self.block, width)),
            scratch=[pltpu.VMEM((self.block, width), F32)],
        )
        got = swap(part, bit, 0)
        self.received.append(([k ^ bit for k in away], start, width, got))
        return got

    def rest(self, start=0, width=None):
        for stage in range(1, len(self.orders[True])):
            got = self.send(stage, start, width)
        return got

    def far(self, start=0, width=None):
        for stage in range(len(self.orders[False]) - 1):
            got = self.send(stage, start, width, False)
        return got

    def near(self, start=0, width=None):
        return self.send(len(self.orders[False]) - 1, start, width, False)

    def whole(self, mask, final, **kwargs):
        extra = [
            (array, masks.index(mask), 0)
            for masks, _, _, array in self.received
            if mask in masks
        ]
        starts = [begin for masks, begin, _, _ in self.received if mask in masks]
        if final:
            extra.append((self.peer, 0, 0))
        return self.call(
            functools.partial(grad_whole_kernel, starts, final), [mask], extra,
            scratch=[pltpu.VMEM((self.block, self.c), F32)], **kwargs,
        )

    def last(self):
        part = self.whole(
            TP_BIT, False,
            grid=(1,),
            out_specs=pl.BlockSpec((None, self.block, self.c), lambda k, at: (0, 0, 0)),
            out_shape=shape_of((1, self.block, self.c)),
        )
        self.peer = swap(part, TP_BIT, 0)

    def finish(self):
        return self.whole(
            0, True,
            grid=(2,),
            out_specs=pl.BlockSpec((self.block, self.c), lambda k, at: (0, k ^ at[2])),
            out_shape=shape_of((self.block, 2 * self.c), F32),
        )


def prepare_kernel(at_ref, q_ref, k_ref, v_ref, out_ref):
    width = k_ref.shape[1] // 2

    def own(ref):
        x = ref[...].astype(F32)
        return jnp.where(at_ref[2] == 0, x[:, :width], x[:, width:])

    x = jnp.concatenate([q_ref[...].astype(F32), own(k_ref), own(v_ref)], axis=1)
    out_ref[...] = x.T.astype(BF)


def prepare(line, w_query, w_key, w_value):
    m = w_query.shape[0]
    width, kv_width = w_query.shape[1] // 2, w_key.shape[1]
    rows = 512
    kv = pl.BlockSpec((rows, kv_width), lambda j, at: (j, 0))
    return line.call(
        prepare_kernel, w_query, w_key, w_value,
        grid=(m // rows,),
        in_specs=[pl.BlockSpec((rows, width), lambda j, at: (j, at[2])), kv, kv],
        out_specs=pl.BlockSpec((width + kv_width, rows), lambda j, at: (0, j)),
        out_shape=shape_of((width + kv_width, m)),
        name="prepare",
    )


def swap(x, narrow_mask, wide_mask):
    wide = lax.axis_size("wide")
    count = lax.axis_size("narrow") * wide
    mask = narrow_mask * wide + wide_mask
    return lax.ppermute(x, AXES, [(d, d ^ mask) for d in range(count)])


def chip_groups():
    wide = lax.axis_size("wide")
    count = lax.axis_size("narrow") * wide
    masks = (0, 2, TP_BIT * wide, TP_BIT * wide + 2)
    groups = sorted({tuple(sorted(d ^ mask for mask in masks)) for d in range(count)})
    return [list(group) for group in groups]


def exchange(x):
    return lax.all_to_all(x, AXES, 0, 0, tiled=True, axis_index_groups=chip_groups())


def gathered(x):
    a = exchange(x)
    return a, swap(a, 0, 1)


def scatter(line, a, b, shape):
    return exchange(chip_sum(line, a, b).reshape(shape))


def row_masks(count):
    return [(k & 1) | ((k >> 1) << 2) for k in range(count // 2)]


class Total:
    def __init__(self, x):
        self.x = x
        narrow = [1 << k for k in range(lax.axis_size("narrow").bit_length() - 1)]
        wide = [1 << k for k in range(lax.axis_size("wide").bit_length() - 1)]
        self.steps = [(0, k) for k in wide] + [(TP_BIT, 0)] + [(k, 0) for k in narrow if k != TP_BIT]

    def step(self, line):
        sent = swap(after(self.x, line.last[0]), *self.steps.pop(0))
        self.x = self.x + sent
        return sent

    def rest(self, line):
        while self.steps:
            self.step(line)
        return self.x


def after(x, *others):
    return lax.optimization_barrier((x, *others))[0]


def unit_rows(v):
    r = lax.rsqrt(jnp.mean(v * v, axis=-1, keepdims=True) + EPS)
    return v * r, r


def shards(
    tokens, lengths, attn_gain, w_query, key_matrix, value_matrix, q_gain, k_gain, w_out, ffn_gain,
    w_gate, w_up, w_down, out_grad,
):
    n, w = lax.axis_index("narrow"), lax.axis_index("wide")
    count = lax.axis_size("narrow")
    share, seqs, m = tokens.shape
    b = share * lax.axis_size("wide")
    half = (n // TP_BIT) % 2

    inside = position_inside(jnp.arange(b, dtype=jnp.int32), share, w)
    positions = jnp.stack([block_of(n, 0, i) * b + inside for i in range(2)]).astype(F32)
    freqs = jnp.exp(-math.log(10000.0) * jnp.arange(HALF, dtype=F32) * 2.0 / HEAD)
    angles = positions[:, None, :] * freqs[None, :, None]
    cos, sin = jnp.cos(angles), jnp.sin(angles)
    qg, kg = q_gain[:, None], k_gain[:, None]
    line = Line(jnp.concatenate([jnp.stack([n, w, half]).astype(jnp.int32), lengths]))
    masks = row_masks(count)
    rows = seqs * b
    shape = (4, seqs, share, m)

    def flat(pair):
        return tuple(x.reshape(rows, x.shape[-1]) for x in pair)

    def whole(pair):
        return tuple((x, 0) for x in flat(pair))

    def halves(x):
        return ((x, 0), (x, 1))

    tok = jnp.moveaxis(tokens, 1, 0)
    out_grad = jnp.moveaxis(out_grad, 1, 0)

    unit, _ = unit_rows(tok.astype(F32))
    sent = exchange(jnp.broadcast_to((unit * attn_gain).astype(BF)[None], shape))
    grad = mask(line, out_grad, b)
    wt = prepare(line, w_query, key_matrix, value_matrix)
    sent = after(sent, wt)
    xn = (sent, swap(sent, 0, 1))
    g_own = exchange(after(grad, sent))
    kv, q, raw = project(line, xn, wt, cos, sin, qg, kg)
    kvs = [swap(kv, k, 0) if k else kv for k in masks]
    xn_turned = turn(line, flat(xn))
    line.wait(g_own)
    pb, pa, oa, ob, log = attend(line, q, kvs, masks, w_out, share)
    pb = swap(pb, 0, 1)
    g_all = (g_own, swap(g_own, 0, 1))
    parts = scatter(line, *flat((pa, pb)), shape)
    g_turned = turn(line, flat(g_all))
    hn, h = middle(line, parts, tok, ffn_gain[None])
    hn = gathered(hn)

    db, da, act, dgate, dup = ffn(line, flat(hn), flat(g_all), w_gate, w_up, w_down)
    db = swap(db, 0, 1)
    c = act.shape[1]
    first, rest = (0, c // 4), (c // 4, 3 * c // 4)
    early, late = (0, 3 * c // 8), (3 * c // 8, 5 * c // 8)
    d_down = WeightGrad(line, g_turned, halves(act))
    d_down.send(0)
    parts = scatter(line, da, db, shape)
    hn_turned = turn(line, flat(hn))
    d_gate = WeightGrad(line, hn_turned, halves(dgate))
    d_up = WeightGrad(line, hn_turned, halves(dup))
    u_first = d_up.far(*early)
    g_first = d_gate.send(0, *first)
    g_rest = d_gate.send(0, *rest)
    dhl, dh, ffn_gain_grad = middle_back(line, parts, h, grad, ffn_gain[None])
    dhl = exchange(dhl)
    line.wait(u_first)
    d_first = d_down.rest(*first)
    yb, ya = down(line, act, w_down)
    yb = swap(yb, 0, 1)
    d_rest = d_down.rest(*rest)
    dhl = after(dhl, line.last[0], g_first, d_first, yb)
    dhl = (dhl, swap(dhl, 0, 1))
    mixed_parts = scatter(line, ya, yb, shape)

    back = attend_back(line, dhl, q, kvs, masks, w_out, (oa, ob), log, raw, cos, sin, qg, share)
    dq, dkvs, dqg = back[:2], after(tuple(back[2:-1]), g_rest, d_rest), back[-1]
    dkvs = [swap(x, k, 0) if k else x for x, k in zip(dkvs, masks)]
    dhl_turned = turn(line, flat(dhl))
    dxb, dxa, dwa, dwb, dkg, dag = project_back(line, dkvs, dq, raw, xn, wt, cos, sin, kg)
    dxb = swap(dxb, 0, 1)
    mixed = finish_mixed(line, mixed_parts, h)
    parts = scatter(line, *flat((dxa, dxb)), shape)
    g_z = d_gate.rest()
    d_up.send(0, *late)
    d_qkv = WeightGrad(line, xn_turned, whole((dwa, dwb)))
    d_qkv.send(0)
    d_out = WeightGrad(line, dhl_turned, whole((oa, ob)))
    d_out.send(0)
    d_up.near(*early)
    gains = jnp.concatenate(
        [dag[0] / attn_gain, ffn_gain_grad[0], jnp.sum(dqg, axis=1), jnp.sum(dkg, axis=1)]
    )
    gains = Total(gains.reshape(-1, 128))
    sent = gains.step(line)
    d_down.last()
    line.wait(g_z, sent)
    d_tokens = finish_tokens(line, parts, tok, dh, attn_gain[None])
    sent = gains.step(line)
    d_qkv.rest()
    d_out.rest()
    u_z = d_up.rest(*late)
    d_gate.last()
    down_grad = d_down.finish()
    line.wait(sent)
    d_qkv.last()
    sent = gains.step(line)
    gate_grad = d_gate.finish()
    line.wait(u_z)
    d_up.last()
    d_out.last()
    line.wait(sent)
    qkv_grad = d_qkv.finish()
    sent = gains.step(line)
    out_grad_t = d_out.finish()
    line.wait(sent)
    up_grad = d_up.finish()
    gains = gains.rest(line).reshape(-1)
    width = dq[0].shape[3]
    columns = dwa.shape[3]
    qkv_grad = qkv_grad.reshape(-1, 2, columns)
    query_grad = qkv_grad[:, :, :width].reshape(-1, 2 * width)
    return (
        jnp.moveaxis(mixed, 0, 1),
        jnp.moveaxis(d_tokens, 0, 1),
        gains[:m],
        query_grad,
        qkv_grad[:, :, width : width + HEAD].reshape(-1, 2 * HEAD),
        qkv_grad[:, :, width + HEAD :].reshape(-1, 2 * HEAD),
        gains[2 * m : 2 * m + HEAD],
        gains[2 * m + HEAD :],
        out_grad_t,
        gains[m : 2 * m],
        gate_grad,
        up_grad,
        down_grad,
    )


def solution(mesh):
    rows = P(AXES, None, None)
    columns = P(None, "wide")
    block = P("narrow", "wide")
    in_specs = (
        rows, P(), P(), columns, columns, columns, P(), P(), P("wide", None), P(), columns, columns,
        P("wide", None), rows,
    )
    out_specs = (
        rows, rows, P(), block, block, block, P(), P(), block, P(), block, block, block,
    )
    return jax.shard_map(shards, mesh=mesh, in_specs=in_specs, out_specs=out_specs, check_vma=False)
```
